512 devices in a mesh: leaf: 32 (over y, x, core), front: 16 (over z).
Axes of the slice: x: 4, y: 4, z: 16, core: 2. Of those that a mesh axis runs over, the one named last changes fastest.
Arguments:
- leaf_pivot_block: bfloat16 [32, 2048, 256], P('leaf', 'front'), may hold values from -6 to 6
- leaf_rest_block: bfloat16 [32, 512, 256], P('leaf', 'front'), may hold values from -6 to 6
- node_pivot_block: bfloat16 [32, 2048, 256], P('leaf', 'front'), may hold values from -6 to 6
- node_rest_block: bfloat16 [32, 512, 256], P('leaf', 'front'), may hold values from -6 to 6
- leaf_vectors_pivot: bfloat16 [32, 2, 2048, 2048], P('leaf', None, 'front'), may hold values from -0.125 to 0.125
- leaf_vectors_rest: bfloat16 [32, 2, 512, 2048], P('leaf', None, 'front'), may hold values from -0.125 to 0.125
- node_vectors_pivot: bfloat16 [32, 2, 2048, 2048], P('leaf', None, 'front'), may hold values from -0.125 to 0.125
- node_vectors_rest: bfloat16 [32, 2, 512, 2048], P('leaf', None, 'front'), may hold values from -0.125 to 0.125
- stack_place: int32 [32, 1024], P('leaf'), may hold values from 0 to 2559, as said below
- parent_columns: int32 [32, 2, 512], P('leaf'), may hold values from 0 to 2047, as said below
- coupling: bfloat16 [32, 2, 2048, 512], P('leaf', None, 'front'), may hold values from -0.125 to 0.125
- pivot_inverse: bfloat16 [32, 2, 2048, 2048], P('leaf', None, 'front'), may hold values from -0.125 to 0.125
Outputs:
- solution: bfloat16 [32, 2, 2048, 256], P('leaf', None, 'front')
- remainder: bfloat16 [32, 512, 256], P('leaf', 'front')
The draws below stay inside these ranges and needn't reach their ends.
Inputs may be any that keep to these rules, and one draw needn't show every extreme that they name: `stack_place`: each group's row holds 1024 distinct stack rows. `parent_columns`: each group's row for each slot holds 512 distinct pivot columns.
All inputs are finite; a program needn't handle non-finite values.
Results may differ from the reference program's by a relative error of at most 0.024.
Values may be sent and summed in bfloat16 or wider, within the bound.
No kernel may reach another device: no remote copies, remote signals or barrier semaphores. Data moves between devices by JAX's collectives and lax.ppermute only.
A program may use at most 64 MiB of HBM per device.

```python
import jax
import jax.numpy as jnp
from jax import lax

K = 2048
C = 512
R = 256
LEVELS = 2
M = 2560
GROUPS = 32
N_FRONT = 16


def draw_stack_place(key, part):
    subkeys = jax.random.split(jax.random.fold_in(key, 17), GROUPS)

    def pick_rows(subkey):
        return jax.random.permutation(subkey, K + C)[:2 * C]
    return jax.vmap(pick_rows)(subkeys).astype(jnp.int32)


def draw_parent_columns(key, part):
    subkeys = jax.random.split(jax.random.fold_in(key, 29), GROUPS * 2)

    def pick_columns(subkey):
        return jax.random.permutation(subkey, K)[:C]
    picked = jax.vmap(pick_columns)(subkeys)
    return picked.reshape(GROUPS, 2, C).astype(jnp.int32)


def shard_levels(own_key, shape, cuts, low, top_value):
    factor_of, own = 1.0, jax.random.fold_in(own_key, 6)
    for dim, parts in cuts:
        heights = jnp.exp(jax.random.uniform(jax.random.fold_in(own, dim), (parts,), jnp.float32, low / len(cuts), top_value / len(cuts)))
        factor_of = factor_of * jnp.repeat(heights, shape[dim] // parts).reshape([-1 if axis == dim else 1 for axis in range(len(shape))])
    return factor_of


def scatter_about(own_key, extent, scale, bound, cuts=(), held_as=jnp.bfloat16):
    gain = shard_levels(own_key, extent, cuts, -0.22, 0.18) if cuts else 1.0
    values = jax.random.normal(own_key, extent, jnp.float32) * scale * gain
    return jnp.minimum(jnp.maximum(values, -bound), bound).astype(held_as)


def setup_inputs(seed: int = 0) -> dict:
    streams_of = jax.random.split(jax.random.key(seed), 13)
    return {
        "leaf_pivot_block": scatter_about(streams_of[0], (GROUPS, K, R), 1.0, 6.0, ((0, 32), (1, 16))),
        "leaf_rest_block": scatter_about(streams_of[1], (GROUPS, C, R), 1.0, 6.0, ((0, 32), (1, 16))),
        "node_pivot_block": scatter_about(streams_of[2], (GROUPS, K, R), 1.0, 6.0, ((0, 32), (1, 16))),
        "node_rest_block": scatter_about(streams_of[3], (GROUPS, C, R), 1.0, 6.0, ((0, 32), (1, 16))),
        "leaf_vectors_pivot": scatter_about(streams_of[4], (GROUPS, 2, K, K), M ** -0.5, 0.125, ((0, 32), (2, 16))),
        "leaf_vectors_rest": scatter_about(streams_of[5], (GROUPS, 2, C, K), M ** -0.5, 0.125, ((0, 32), (2, 16))),
        "node_vectors_pivot": scatter_about(streams_of[6], (GROUPS, 2, K, K), M ** -0.5, 0.125, ((0, 32), (2, 16))),
        "node_vectors_rest": scatter_about(streams_of[7], (GROUPS, 2, C, K), M ** -0.5, 0.125, ((0, 32), (2, 16))),
        "stack_place": draw_stack_place(jax.random.fold_in(streams_of[12], 71), 0),
        "parent_columns": draw_parent_columns(jax.random.fold_in(streams_of[12], 71), 0),
        "coupling": scatter_about(streams_of[10], (GROUPS, 2, K, C), (4 * C) ** -0.5, 0.125, ((0, 32), (2, 16))),
        "pivot_inverse": scatter_about(streams_of[11], (GROUPS, 2, K, K), K ** -0.5, 0.125, ((0, 32), (2, 16))),
    }


def reflect(block_pivot, block_rest, vectors_pivot, vectors_rest):
    blocks = N_FRONT

    def partials(vectors, values):
        count = vectors.shape[1]
        left_side = vectors[1].reshape(blocks, count // blocks, K).astype(jnp.float32)
        right_side = values.reshape(blocks, count // blocks, R).astype(jnp.float32)
        return jnp.einsum("bik,bir->bkr", left_side, right_side)

    partial_value = partials(vectors_pivot, block_pivot) + partials(vectors_rest, block_rest)
    rounded = lax.optimization_barrier(partial_value.astype(jnp.bfloat16)).astype(jnp.float32)
    summed = jnp.sum(rounded, axis=0).astype(jnp.bfloat16)
    pivots = block_pivot.astype(jnp.float32) - jnp.dot(vectors_pivot[0], summed, preferred_element_type=jnp.float32)
    rest = block_rest.astype(jnp.float32) - jnp.dot(vectors_rest[0], summed, preferred_element_type=jnp.float32)
    return pivots.astype(jnp.bfloat16), rest.astype(jnp.bfloat16)


def reflect_all(block_pivot, block_rest, vectors_pivot, vectors_rest):
    def one_group(items):
        return reflect(items[0], items[1], items[2], items[3])

    return lax.map(one_group, (block_pivot, block_rest, vectors_pivot, vectors_rest))


def shifted(values, amount):
    if amount == 0:
        return values
    return jnp.roll(values, amount, axis=0)


def added(first, second):
    return (first.astype(jnp.float32) + second.astype(jnp.float32)).astype(jnp.bfloat16)


def reference(leaf_pivot_block, leaf_rest_block, node_pivot_block, node_rest_block, leaf_vectors_pivot, leaf_vectors_rest, node_vectors_pivot, node_vectors_rest, stack_place, parent_columns, coupling, pivot_inverse):
    subtree = 2 ** LEVELS
    leaf_pivots, leaf_remainder = reflect_all(leaf_pivot_block, leaf_rest_block, leaf_vectors_pivot, leaf_vectors_rest)

    def run_nodes(left_part, right_part):
        def place(own_pivot, own_rest, rows, left_one, right_one):
            joined = jnp.concatenate([left_one, right_one], axis=0)
            stack = jnp.concatenate([own_pivot, own_rest], axis=0)
            stack = stack.at[rows].set(joined)
            return stack[:K], stack[K:]

        stack_pivots, stack_rest = jax.vmap(place)(node_pivot_block, node_rest_block, stack_place, left_part, right_part)
        return reflect_all(stack_pivots, stack_rest, node_vectors_pivot, node_vectors_rest)

    node_pivots, node_remainder = run_nodes(shifted(leaf_remainder, 1), leaf_remainder)
    for height in range(2, LEVELS + 1):
        offset = 2 ** (height - 2)
        node_pivots, node_remainder = run_nodes(shifted(node_remainder, offset), shifted(node_remainder, -offset))
    root_part = shifted(node_remainder, -(subtree // 2))
    node_pivots, node_remainder = run_nodes(root_part, jnp.zeros_like(root_part))

    def settle_all(pivots, which_slot, parent):
        def one_group(own, columns, couple, inverse, parent_one):
            right_side = own.astype(jnp.float32)
            if parent_one is not None:
                chosen = parent_one[columns]
                right_side = right_side - jnp.dot(couple, chosen, preferred_element_type=jnp.float32)
            result = jnp.dot(inverse, right_side.astype(jnp.bfloat16), preferred_element_type=jnp.float32)
            return result.astype(jnp.bfloat16)

        if parent is None:
            return jax.vmap(lambda own, inverse: one_group(own, None, None, inverse, None))(pivots, pivot_inverse[:, which_slot])
        return jax.vmap(one_group)(pivots, parent_columns[:, which_slot], coupling[:, which_slot], pivot_inverse[:, which_slot], parent)

    node_solution = settle_all(node_pivots, 1, None)
    for height in range(LEVELS, 0, -1):
        if height == LEVELS:
            parent_part = shifted(node_solution, subtree // 2)
        else:
            offset = 2 ** (height - 1)
            parent_part = added(shifted(node_solution, -offset), shifted(node_solution, offset))
        node_solution = settle_all(node_pivots, 1, parent_part)
    parent_part = added(shifted(node_solution, -1), node_solution)
    leaf_solution = settle_all(leaf_pivots, 0, parent_part)
    solution = jnp.stack([leaf_solution, node_solution], axis=1)
    return solution, node_remainder
```

```python
import jax
import jax.numpy as jnp
from jax import lax
from jax.sharding import Mesh
from jax.sharding import PartitionSpec as P

LEVELS = 2
FRONT = ("fa", "fb")
BF16 = jnp.bfloat16
F32 = jnp.float32


def mm(spec, a, b):
    return jnp.einsum(spec, a, b, preferred_element_type=F32)


def from_behind(block, distance):
    count = lax.axis_size("leaf")
    return lax.ppermute(block, "leaf", [((i - distance) % count, i) for i in range(count)])


def exchange(parts, axis):
    return lax.all_to_all(parts, axis, split_axis=0, concat_axis=0, tiled=True)


def to_all(block, axis):
    count = 1
    for name in (axis,) if isinstance(axis, str) else axis:
        count *= lax.axis_size(name)
    return exchange(jnp.broadcast_to(block, (count, *block.shape)), axis)


def total(parts):
    return jnp.sum(parts.astype(F32), axis=0)


def added(first, second):
    return (first.astype(F32) + second.astype(F32)).astype(BF16)


def folded(block):
    half = block.shape[0] // 2
    return jnp.concatenate([block[:half], block[half:]], axis=1)


def unfolded(blocks):
    half = blocks.shape[-1] // 2
    return jnp.concatenate([blocks[..., :half], blocks[..., half:]], axis=-2)


def per_device(
    leaf_pivot_block,
    leaf_rest_block,
    node_pivot_block,
    node_rest_block,
    leaf_vectors_pivot,
    leaf_vectors_rest,
    node_vectors_pivot,
    node_vectors_rest,
    stack_place,
    parent_columns,
    coupling,
    pivot_inverse,
):
    na, nb = lax.axis_size("fa"), lax.axis_size("fb")
    fronts = na * nb
    ia, ib = lax.axis_index("fa"), lax.axis_index("fb")
    me = ia * nb + ib
    kp = leaf_vectors_pivot.shape[2]
    kc = leaf_vectors_rest.shape[2]
    ks = kp + kc
    K, C = kp * fronts, kc * fronts
    R = leaf_pivot_block.shape[2]
    rc = R // fronts
    place = stack_place[0]
    subtree = 2**LEVELS

    def stack_rows(device):
        device = jnp.asarray(device, jnp.int32)
        return jnp.concatenate(
            [
                device * kp + jnp.arange(kp, dtype=jnp.int32),
                K + device * kc + jnp.arange(kc, dtype=jnp.int32),
            ]
        )

    ve_blocks = jnp.concatenate(jnp.split(node_vectors_rest[0, 0], K // C, axis=1), axis=0)
    gathered = lax.all_gather(jnp.concatenate([ve_blocks, coupling[0, 1]], axis=0), FRONT, axis=0)
    ve_all = gathered[:, : kc * (K // C)].reshape(fronts, K // C, kc, C)
    coupling_all = gathered[:, kc * (K // C) :].reshape(K, C)

    node_w = jnp.concatenate([node_vectors_pivot[0, 1], node_vectors_rest[0, 1]], axis=0)
    node_v = jnp.concatenate([node_vectors_pivot[0, 0], node_vectors_rest[0, 0]], axis=0)
    rows = stack_rows(me)
    unit = (rows[:, None] == K + jnp.arange(C, dtype=jnp.int32)[None]).astype(F32)
    product = mm("sbk,dbck->sdc", node_w.reshape(ks, K // C, C), ve_all).reshape(ks, C)
    section_rows = (unit - product).astype(BF16)
    node_reach = mm("pm,mc->pc", pivot_inverse[0, 1], coupling_all).astype(BF16)
    gathered = lax.all_gather(jnp.concatenate([section_rows, node_reach], axis=0), FRONT, axis=0)
    section_all = gathered[:, :ks].reshape(fronts * ks, C)
    node_reach_all = gathered[:, ks:].reshape(K, C)

    leaf_partial = mm("ik,ir->kr", leaf_vectors_pivot[0, 1], leaf_pivot_block[0])
    leaf_partial = leaf_partial + mm("ik,ir->kr", leaf_vectors_rest[0, 1], leaf_rest_block[0])
    part = exchange(leaf_partial.astype(BF16).reshape(nb, K // nb, R), "fb")
    part = exchange(total(part).astype(BF16).reshape(na, kp, R), "fa")
    leaf_y = to_all(to_all(total(part).astype(BF16), "fa").reshape(K // nb, R), "fb").reshape(K, R)
    leaf_pivots = (leaf_pivot_block[0] - mm("pk,kr->pr", leaf_vectors_pivot[0, 0], leaf_y)).astype(BF16)
    leaf_rest = (leaf_rest_block[0] - mm("pk,kr->pr", leaf_vectors_rest[0, 0], leaf_y)).astype(BF16)

    own_hit = rows[:, None] == place[None]
    own = jnp.concatenate([node_pivot_block[0], node_rest_block[0]], axis=0)
    own = jnp.where(jnp.any(own_hit, axis=1)[:, None], jnp.zeros_like(own), own)

    both = jnp.concatenate([leaf_rest, own], axis=0).T.reshape(fronts, rc, kc + ks)
    both = exchange(both, FRONT)
    rest = both[:, :, :kc].transpose(1, 0, 2).reshape(rc, C)
    own_columns = both[:, :, kc:].transpose(1, 0, 2).reshape(rc, fronts * ks)

    blocks = jnp.concatenate([node_w, node_v], axis=0).reshape(2 * ks, nb, K // nb).transpose(1, 0, 2)
    own_folded = folded(own)
    blocks = jnp.concatenate([blocks, jnp.broadcast_to(own_folded, (nb, *own_folded.shape))], axis=1)
    blocks = exchange(blocks, "fb")
    w_block = blocks[:, :ks].reshape(nb * ks, K // nb)
    v_block = blocks[:, ks : 2 * ks].reshape(nb * ks, K // nb)
    own_block = unfolded(blocks[:, 2 * ks :]).reshape(nb * ks, R)
    inverse_block = pivot_inverse[0, 1].reshape(kp, na, K // na).transpose(1, 0, 2)
    inverse_block = exchange(inverse_block, "fa").reshape(na * kp, K // na)
    block_rows = jnp.concatenate([stack_rows(ia * nb + b) for b in range(nb)])
    block_hit = (place[:C, None] == block_rows[None]).astype(BF16)
    w_left = mm("cs,sk->ck", block_hit, w_block).astype(BF16)
    y_own = mm("sr,sk->rk", own_block, w_block)

    device = jnp.where(place < K, place // kp, (place - K) // kc)
    within = jnp.where(place < K, place % kp, kp + (place - K) % kc)
    section_map = jnp.take(section_all, device * ks + within, axis=0)
    section_own = mm("rs,sc->rc", own_columns, section_all)

    def section(left, right):
        children = jnp.concatenate([left, right], axis=1)
        return (section_own + mm("rj,jc->rc", children, section_map)).astype(BF16)

    rest = section(from_behind(rest, 1), rest)
    rest = section(from_behind(rest, 1), from_behind(rest, -1))
    left = to_all(from_behind(rest, -(subtree // 2)), FRONT).reshape(R, C)

    partial_y = (y_own + mm("rc,ck->rk", left, w_left)).astype(BF16)
    part = total(exchange(partial_y.reshape(na, R // na, K // nb), "fa")).astype(BF16)
    y_block = to_all(part, "fa").reshape(R, K // nb)
    part = mm("sk,rk->sr", v_block, y_block).astype(BF16).reshape(nb, ks, R)
    placed = mm("sc,rc->sr", own_hit[:, :C].astype(BF16), left)
    reflected = own.astype(F32) + placed - total(exchange(part, "fb"))
    reflected = reflected.astype(BF16)
    remainder = reflected[kp:]
    pivots = to_all(reflected[:kp], "fb").reshape(nb * kp, R)
    part = mm("mr,pm->rp", pivots, inverse_block).astype(BF16)
    part = total(exchange(part.reshape(na, R // na, na * kp), "fa")).astype(BF16)
    part = exchange(part.reshape(nb, rc, na * kp), "fb")
    top = part.reshape(nb, rc, na, kp).transpose(1, 2, 0, 3).reshape(rc, K)

    wide = jnp.concatenate([coupling[0, 0], folded(leaf_pivots)], axis=0)
    wide, gathered = lax.optimization_barrier((wide, gathered))
    gathered_leaf = lax.all_gather(wide, FRONT, axis=0)
    leaf_coupling_all = gathered_leaf[:, :kp].reshape(K, C)
    leaf_pivots_all = unfolded(gathered_leaf[:, kp:]).reshape(K, R)
    leaf_reach = mm("pm,mc->pc", pivot_inverse[0, 0], leaf_coupling_all).astype(BF16)
    leaf_own = mm("pm,mr->pr", pivot_inverse[0, 0], leaf_pivots_all).astype(BF16)
    wide = jnp.concatenate([leaf_reach, folded(leaf_own)], axis=0)
    gathered_leaf = lax.all_gather(wide, FRONT, axis=0)
    leaf_reach_all = gathered_leaf[:, :kp].reshape(K, C)
    leaf_own_all = unfolded(gathered_leaf[:, kp:]).reshape(K, R)
    mine = (me * rc + jnp.arange(rc, dtype=jnp.int32))[:, None] == jnp.arange(R, dtype=jnp.int32)[None]
    leaf_own_columns = mm("qr,pr->qp", mine.astype(BF16), leaf_own_all)

    pivot_ids = jnp.arange(K, dtype=jnp.int32)[:, None]
    node_pick = (pivot_ids == parent_columns[0, 1][None]).astype(BF16)
    leaf_pick = (pivot_ids == parent_columns[0, 0][None]).astype(BF16)

    def settle(base, parent, pick, reach):
        chosen = mm("rp,pc->rc", parent, pick).astype(BF16)
        return (base - mm("rc,pc->rp", chosen, reach)).astype(BF16)

    node = top
    for height in range(LEVELS, 0, -1):
        if height == LEVELS:
            parent = from_behind(node, subtree // 2)
        else:
            offset = 2 ** (height - 1)
            parent = added(from_behind(node, -offset), from_behind(node, offset))
        node = settle(top.astype(F32), parent, node_pick, node_reach_all)
    parent = added(from_behind(node, -1), node)
    leaf = settle(leaf_own_columns, parent, leaf_pick, leaf_reach_all)
    both = jnp.stack([leaf, node]).reshape(2, rc, fronts, kp).transpose(2, 0, 1, 3)
    both = exchange(both, FRONT)
    both = both.transpose(1, 3, 0, 2).reshape(2, kp, R)
    return (both[None], remainder[None])


def solution(mesh):
    leaves, fronts = mesh.devices.shape
    nb = next(n for n in range(max(1, int(fronts**0.5)), 0, -1) if fronts % n == 0)
    grid = Mesh(mesh.devices.reshape(leaves, fronts // nb, nb), ("leaf", "fa", "fb"))
    rows3 = P("leaf", FRONT, None)
    rows4 = P("leaf", None, FRONT, None)
    in_specs = (
        *([rows3] * 4),
        *([rows4] * 4),
        P("leaf", None),
        P("leaf", None, None),
        rows4,
        rows4,
    )
    return jax.shard_map(
        per_device, mesh=grid, in_specs=in_specs, out_specs=(rows4, rows3), check_vma=False
    )
```

```python
import jax
import jax.numpy as jnp
from jax import lax
from jax.sharding import Mesh
from jax.sharding import PartitionSpec as P

LEVELS = 2
FRONT = ("fa", "fb")
BF16 = jnp.bfloat16
F32 = jnp.float32


def mm(spec, a, b):
    return jnp.einsum(spec, a, b, preferred_element_type=F32)


def from_behind(block, distance):
    count = lax.axis_size("leaf")
    return lax.ppermute(block, "leaf", [((i - distance) % count, i) for i in range(count)])


def exchange(parts, axis):
    return lax.all_to_all(parts, axis, split_axis=0, concat_axis=0, tiled=True)


def to_all(block, axis):
    count = 1
    for name in (axis,) if isinstance(axis, str) else axis:
        count *= lax.axis_size(name)
    return exchange(jnp.broadcast_to(block, (count, *block.shape)), axis)


def total(parts):
    return jnp.sum(parts.astype(F32), axis=0)


def after(block, earlier):
    corner = earlier[(0,) * (earlier.ndim - 1) + (slice(0, 1),)]
    return block + (corner * 0).astype(block.dtype)


def added(first, second):
    return (first.astype(F32) + second.astype(F32)).astype(BF16)


def folded(block):
    half = block.shape[0] // 2
    return jnp.concatenate([block[:half], block[half:]], axis=1)


def unfolded(blocks):
    half = blocks.shape[-1] // 2
    return jnp.concatenate([blocks[..., :half], blocks[..., half:]], axis=-2)


def per_device(
    leaf_pivot_block,
    leaf_rest_block,
    node_pivot_block,
    node_rest_block,
    leaf_vectors_pivot,
    leaf_vectors_rest,
    node_vectors_pivot,
    node_vectors_rest,
    stack_place,
    parent_columns,
    coupling,
    pivot_inverse,
):
    na, nb = lax.axis_size("fa"), lax.axis_size("fb")
    fronts = na * nb
    ia, ib = lax.axis_index("fa"), lax.axis_index("fb")
    me = ia * nb + ib
    kp = leaf_vectors_pivot.shape[2]
    kc = leaf_vectors_rest.shape[2]
    ks = kp + kc
    K, C = kp * fronts, kc * fronts
    R = leaf_pivot_block.shape[2]
    rc = R // fronts
    place = stack_place[0]
    subtree = 2**LEVELS

    def stack_rows(device):
        device = jnp.asarray(device, jnp.int32)
        return jnp.concatenate(
            [
                device * kp + jnp.arange(kp, dtype=jnp.int32),
                K + device * kc + jnp.arange(kc, dtype=jnp.int32),
            ]
        )

    node_w = jnp.concatenate([node_vectors_pivot[0, 1], node_vectors_rest[0, 1]], axis=0)
    node_v = jnp.concatenate([node_vectors_pivot[0, 0], node_vectors_rest[0, 0]], axis=0)
    rows = stack_rows(me)

    own_hit = rows[:, None] == place[None]
    own = jnp.concatenate([node_pivot_block[0], node_rest_block[0]], axis=0)
    own = jnp.where(jnp.any(own_hit, axis=1)[:, None], jnp.zeros_like(own), own)

    blocks = jnp.concatenate([node_w, node_v], axis=0).reshape(2 * ks, nb, K // nb).transpose(1, 0, 2)
    own_folded = folded(own)
    blocks = jnp.concatenate([blocks, jnp.broadcast_to(own_folded, (nb, *own_folded.shape))], axis=1)
    blocks = exchange(blocks, "fb")
    w_block = blocks[:, :ks].reshape(nb * ks, K // nb)
    v_block = blocks[:, ks : 2 * ks].reshape(nb * ks, K // nb)
    own_block = unfolded(blocks[:, 2 * ks :]).reshape(nb * ks, R)

    ve_block = to_all(blocks[:, ks + kp : 2 * ks], "fa").reshape(C, K // nb)
    product = mm("sk,ck->sc", w_block, ve_block).astype(BF16).reshape(nb, ks, C)
    product = total(exchange(product, "fb"))
    unit = (rows[:, None] == K + jnp.arange(C, dtype=jnp.int32)[None]).astype(F32)
    section_rows = (unit - product).astype(BF16)

    leaf_ve = jnp.concatenate(jnp.split(leaf_vectors_rest[0, 0], K // C, axis=1), axis=0)
    gathered = lax.all_gather(jnp.concatenate([section_rows, leaf_ve], axis=0), FRONT, axis=0)
    section_all = gathered[:, :ks].reshape(fronts * ks, C)
    leaf_ve_all = gathered[:, ks:].reshape(fronts, K // C, kc, C)

    leaf_partial = mm("ik,ir->rk", leaf_vectors_pivot[0, 1], leaf_pivot_block[0])
    leaf_partial = leaf_partial + mm("ik,ir->rk", leaf_vectors_rest[0, 1], leaf_rest_block[0])
    part = after(leaf_partial, product).astype(BF16).reshape(nb, R // nb, K)
    part = total(exchange(part, "fb")).astype(BF16)
    leaf_y = total(exchange(part.reshape(na, rc, K), "fa")).astype(BF16)
    both = jnp.concatenate([leaf_rest_block[0], own], axis=0).T.reshape(nb, na, rc, kc + ks)
    both = both.transpose(1, 0, 2, 3).reshape(fronts, rc, kc + ks)
    both = exchange(both, FRONT)
    leaf_rest = both[:, :, :kc].transpose(1, 0, 2).reshape(rc, C)
    own_columns = both[:, :, kc:].transpose(1, 0, 2).reshape(rc, fronts * ks)

    inverse_block = pivot_inverse[0, 1].reshape(kp, na, nb, kp).transpose(2, 0, 1, 3)
    inverse_block = exchange(inverse_block.reshape(nb, kp, na * kp), "fb")
    inverse_block = inverse_block.reshape(nb * kp, na * kp)
    block_rows = jnp.concatenate([stack_rows(ia * nb + b) for b in range(nb)])
    block_hit = (place[:C, None] == block_rows[None]).astype(BF16)
    w_left = mm("cs,sk->ck", block_hit, w_block).astype(BF16)
    y_own = mm("sr,sk->rk", own_block, w_block)

    rest = mm("rbk,dbck->rdc", leaf_y.reshape(rc, K // C, C), leaf_ve_all).reshape(rc, C)
    rest = (after(leaf_rest, inverse_block) - rest).astype(BF16)

    y_folded = jnp.concatenate(jnp.split(leaf_y, K // C, axis=1), axis=0)
    wide = jnp.concatenate([coupling[0, 1], coupling[0, 0], y_folded], axis=0)
    gathered = lax.all_gather(after(wide, inverse_block), FRONT, axis=0)
    node_coupling_all = gathered[:, :kp].reshape(K, C)
    leaf_coupling_all = gathered[:, kp : 2 * kp].reshape(K, C)
    leaf_y_all = gathered[:, 2 * kp :].reshape(na, nb, K // C, rc, C).transpose(1, 0, 3, 2, 4)
    leaf_y_all = leaf_y_all.reshape(R, K)
    node_reach = mm("pm,mc->pc", pivot_inverse[0, 1], node_coupling_all).astype(BF16)
    leaf_reach = mm("pm,mc->pc", pivot_inverse[0, 0], leaf_coupling_all).astype(BF16)
    leaf_pivots = leaf_pivot_block[0] - mm("pk,rk->pr", leaf_vectors_pivot[0, 0], leaf_y_all)
    device = jnp.where(place < K, place // kp, (place - K) // kc)
    within = jnp.where(place < K, place % kp, kp + (place - K) % kc)
    section_map = jnp.take(section_all, device * ks + within, axis=0)
    section_own = mm("rs,sc->rc", own_columns, section_all)

    def section(left, right):
        children = jnp.concatenate([left, right], axis=1)
        return (section_own + mm("rj,jc->rc", children, section_map)).astype(BF16)

    rest = section(from_behind(rest, 1), rest)
    rest = section(from_behind(rest, 1), from_behind(rest, -1))
    left = to_all(from_behind(rest, -(subtree // 2)), FRONT)
    left = left.reshape(na, nb, rc, C).transpose(1, 0, 2, 3).reshape(R, C)

    partial_y = (y_own + mm("rc,ck->rk", left, w_left)).astype(BF16)
    part = total(exchange(partial_y.reshape(na, R // na, K // nb), "fa")).astype(BF16)
    y_block = to_all(part, "fa").reshape(R, K // nb)
    part = mm("sk,rk->sr", v_block, y_block).astype(BF16).reshape(nb, ks, R)
    placed = mm("sc,rc->sr", own_hit[:, :C].astype(BF16), left)
    reflected = own.astype(F32) + placed - total(exchange(part, "fb"))
    reflected = reflected.astype(BF16)
    remainder = reflected[kp:]
    pivots = to_all(reflected[:kp], "fa").reshape(na * kp, R)
    part = mm("mr,pm->rp", pivots, inverse_block).astype(BF16)
    part = total(exchange(part.reshape(nb, R // nb, nb * kp), "fb")).astype(BF16)
    part = exchange(part.reshape(na, rc, nb * kp), "fa")
    top = part.transpose(1, 0, 2).reshape(rc, K)

    wide = jnp.concatenate([node_reach, leaf_reach, folded(leaf_pivots.astype(BF16))], axis=0)
    gathered = lax.all_gather(after(wide, y_block), FRONT, axis=0)
    node_reach_all = gathered[:, :kp].reshape(K, C)
    leaf_reach_all = gathered[:, kp : 2 * kp].reshape(K, C)
    leaf_pivots_all = unfolded(gathered[:, 2 * kp :]).reshape(K, R)
    leaf_own = mm("pm,mr->pr", pivot_inverse[0, 0], leaf_pivots_all)

    pivot_ids = jnp.arange(K, dtype=jnp.int32)[:, None]
    node_pick = (pivot_ids == parent_columns[0, 1][None]).astype(BF16)
    leaf_pick = (pivot_ids == parent_columns[0, 0][None]).astype(BF16)

    def reached(parent, pick, reach):
        chosen = mm("rp,pc->rc", parent, pick).astype(BF16)
        return mm("rc,pc->rp", chosen, reach)

    node = top
    for height in range(LEVELS, 0, -1):
        if height == LEVELS:
            parent = from_behind(node, subtree // 2)
        else:
            offset = 2 ** (height - 1)
            parent = added(from_behind(node, -offset), from_behind(node, offset))
        node = (top - reached(parent, node_pick, node_reach_all)).astype(BF16)
    parent = added(from_behind(node, -1), node)
    leaf = reached(parent, leaf_pick, leaf_reach_all).astype(BF16)
    both = jnp.stack([leaf, node]).reshape(2, rc, fronts, kp).transpose(2, 0, 1, 3)
    both = exchange(both, FRONT).reshape(na, nb, 2, rc, kp)
    both = both.transpose(2, 4, 1, 0, 3).reshape(2, kp, R)
    leaf = (leaf_own - both[0]).astype(BF16)
    return (jnp.stack([leaf, both[1]])[None], remainder[None])


def solution(mesh):
    leaves, fronts = mesh.devices.shape
    nb = next(n for n in range(max(1, int(fronts**0.5)), 0, -1) if fronts % n == 0)
    grid = Mesh(mesh.devices.reshape(leaves, fronts // nb, nb), ("leaf", "fa", "fb"))
    rows3 = P("leaf", FRONT, None)
    rows4 = P("leaf", None, FRONT, None)
    in_specs = (
        *([rows3] * 4),
        *([rows4] * 4),
        P("leaf", None),
        P("leaf", None, None),
        rows4,
        rows4,
    )
    return jax.shard_map(
        per_device, mesh=grid, in_specs=in_specs, out_specs=(rows4, rows3), check_vma=False
    )
```

```python
import jax
import jax.numpy as jnp
from jax import lax
from jax.sharding import Mesh
from jax.sharding import PartitionSpec as P

LEVELS = 2
FRONT = ("fa", "fb")
BF16 = jnp.bfloat16
F32 = jnp.float32


def mm(spec, a, b):
    return jnp.einsum(spec, a, b, preferred_element_type=F32)


def from_behind(block, distance):
    count = lax.axis_size("leaf")
    return lax.ppermute(block, "leaf", [((i - distance) % count, i) for i in range(count)])


def exchange(parts, axis):
    return lax.all_to_all(parts, axis, split_axis=0, concat_axis=0, tiled=True)


def to_all(block, axis):
    count = 1
    for name in (axis,) if isinstance(axis, str) else axis:
        count *= lax.axis_size(name)
    return exchange(jnp.broadcast_to(block, (count, *block.shape)), axis)


def total(parts):
    return jnp.sum(parts.astype(F32), axis=0)


def after(block, earlier):
    corner = earlier[(0,) * (earlier.ndim - 1) + (slice(0, 1),)]
    return block + (corner * 0).astype(block.dtype)


def added(first, second):
    return (first.astype(F32) + second.astype(F32)).astype(BF16)


def folded(block):
    half = block.shape[0] // 2
    return jnp.concatenate([block[:half], block[half:]], axis=1)


def unfolded(blocks):
    half = blocks.shape[-1] // 2
    return jnp.concatenate([blocks[..., :half], blocks[..., half:]], axis=-2)


def per_device(
    leaf_pivot_block,
    leaf_rest_block,
    node_pivot_block,
    node_rest_block,
    leaf_vectors_pivot,
    leaf_vectors_rest,
    node_vectors_pivot,
    node_vectors_rest,
    stack_place,
    parent_columns,
    coupling,
    pivot_inverse,
):
    na, nb = lax.axis_size("fa"), lax.axis_size("fb")
    fronts = na * nb
    ia, ib = lax.axis_index("fa"), lax.axis_index("fb")
    me = ia * nb + ib
    kp = leaf_vectors_pivot.shape[2]
    kc = leaf_vectors_rest.shape[2]
    ks = kp + kc
    K, C = kp * fronts, kc * fronts
    R = leaf_pivot_block.shape[2]
    rc = R // fronts
    place = stack_place[0]
    subtree = 2**LEVELS

    def stack_rows(device):
        device = jnp.asarray(device, jnp.int32)
        return jnp.concatenate(
            [
                device * kp + jnp.arange(kp, dtype=jnp.int32),
                K + device * kc + jnp.arange(kc, dtype=jnp.int32),
            ]
        )

    node_w = jnp.concatenate([node_vectors_pivot[0, 1], node_vectors_rest[0, 1]], axis=0)
    node_v = jnp.concatenate([node_vectors_pivot[0, 0], node_vectors_rest[0, 0]], axis=0)
    rows = stack_rows(me)

    own_hit = rows[:, None] == place[None]
    own = jnp.concatenate([node_pivot_block[0], node_rest_block[0]], axis=0)
    own = jnp.where(jnp.any(own_hit, axis=1)[:, None], jnp.zeros_like(own), own)

    node_ve_all = lax.all_gather(node_vectors_rest[0, 0], FRONT, axis=0, tiled=True)

    leaf_partial = mm("ik,ir->kr", leaf_vectors_pivot[0, 1], leaf_pivot_block[0])
    leaf_partial = leaf_partial + mm("ik,ir->kr", leaf_vectors_rest[0, 1], leaf_rest_block[0])
    part = exchange(leaf_partial.astype(BF16).reshape(nb, K // nb, R), "fb")
    part = exchange(total(part).astype(BF16).reshape(na, kp, R), "fa")
    leaf_y = total(part).astype(BF16)

    both = jnp.concatenate([leaf_rest_block[0], own], axis=0).T.reshape(nb, na, rc, kc + ks)
    leaf_ve = leaf_vectors_rest[0, 0].reshape(kc // rc, rc, nb, na, kp).transpose(2, 3, 1, 0, 4)
    leaf_ve = leaf_ve.reshape(nb, na, rc, kc // rc * kp)
    both = jnp.concatenate([both, leaf_ve], axis=3).transpose(1, 0, 2, 3)
    both = exchange(both.reshape(fronts, rc, both.shape[3]), FRONT)
    leaf_rest = both[:, :, :kc].transpose(1, 0, 2).reshape(rc, C)
    own_columns = both[:, :, kc : kc + ks].transpose(1, 0, 2).reshape(rc, fronts * ks)
    leaf_ve = both[:, :, kc + ks :].reshape(fronts, rc, kc // rc, kp).transpose(0, 2, 1, 3).reshape(C, kp)
    part = mm("kr,ck->rc", leaf_y, leaf_ve).astype(BF16)
    part = part.reshape(nb, na, rc, C).transpose(1, 0, 2, 3).reshape(fronts, rc, C)
    rest = (leaf_rest - total(exchange(part, FRONT))).astype(BF16)

    product = mm("sk,ck->sc", node_w, node_ve_all)
    unit = (rows[:, None] == K + jnp.arange(C, dtype=jnp.int32)[None]).astype(F32)
    section_rows = (after(unit, leaf_y) - product).astype(BF16)

    gathered = lax.all_gather(jnp.concatenate([section_rows, coupling[0, 1]], axis=0), FRONT, axis=0)
    section_all = gathered[:, :ks].reshape(fronts * ks, C)
    node_coupling_all = gathered[:, ks:].reshape(K, C)

    blocks = jnp.concatenate([node_w, node_v], axis=0).reshape(2 * ks, nb, K // nb).transpose(1, 0, 2)
    own_folded = folded(own)
    blocks = jnp.concatenate([blocks, jnp.broadcast_to(own_folded, (nb, *own_folded.shape))], axis=1)
    blocks = exchange(after(blocks, rest), "fb")
    w_block = blocks[:, :ks].reshape(nb * ks, K // nb)
    v_block = blocks[:, ks : 2 * ks].reshape(nb * ks, K // nb)
    own_block = unfolded(blocks[:, 2 * ks :]).reshape(nb * ks, R)

    inverse_block = pivot_inverse[0, 1].reshape(kp, na, nb, kp).transpose(2, 0, 1, 3)
    inverse_block = exchange(inverse_block.reshape(nb, kp, na * kp), "fb")
    inverse_block = inverse_block.reshape(nb * kp, na * kp)
    block_rows = jnp.concatenate([stack_rows(ia * nb + b) for b in range(nb)])
    block_hit = (place[:C, None] == block_rows[None]).astype(BF16)
    w_left = mm("cs,sk->ck", block_hit, w_block).astype(BF16)
    y_own = mm("sr,sk->rk", own_block, w_block)

    rest = after(rest, inverse_block)
    node_reach = mm("pm,mc->pc", after(pivot_inverse[0, 1], rest), node_coupling_all).astype(BF16)
    wide = jnp.concatenate([node_reach, coupling[0, 0], folded(leaf_y)], axis=0)
    gathered = lax.all_gather(wide, FRONT, axis=0)
    node_reach_all = gathered[:, :kp].reshape(K, C)
    leaf_coupling_all = gathered[:, kp : 2 * kp].reshape(K, C)
    leaf_y_all = unfolded(gathered[:, 2 * kp :]).reshape(na, nb, kp, R).transpose(1, 0, 2, 3).reshape(K, R)

    device = jnp.where(place < K, place // kp, (place - K) // kc)
    within = jnp.where(place < K, place % kp, kp + (place - K) % kc)
    section_map = jnp.take(section_all, after(device * ks + within, rest[0]), axis=0)
    section_own = mm("rs,sc->rc", after(own_columns, rest), section_all)

    def section(left, right):
        children = jnp.concatenate([left, right], axis=1)
        return (section_own + mm("rj,jc->rc", children, section_map)).astype(BF16)

    rest = section(from_behind(rest, 1), rest)
    rest = section(from_behind(rest, 1), from_behind(rest, -1))
    left = to_all(from_behind(rest, -(subtree // 2)), FRONT)
    left = left.reshape(na, nb, rc, C).transpose(1, 0, 2, 3).reshape(R, C)

    partial_y = (y_own + mm("rc,ck->rk", left, w_left)).astype(BF16)
    part = total(exchange(partial_y.reshape(na, R // na, K // nb), "fa")).astype(BF16)
    y_block = to_all(part, "fa").reshape(R, K // nb)
    part = mm("sk,rk->sr", v_block, y_block).astype(BF16).reshape(nb, ks, R)
    placed = mm("sc,rc->sr", own_hit[:, :C].astype(BF16), left)
    reflected = own.astype(F32) + placed - total(exchange(part, "fb"))
    reflected = reflected.astype(BF16)
    remainder = reflected[kp:]
    pivots = to_all(reflected[:kp], "fa").reshape(na * kp, R)
    part = mm("mr,pm->rp", pivots, inverse_block).astype(BF16)
    part = total(exchange(part.reshape(nb, R // nb, nb * kp), "fb")).astype(BF16)
    part = exchange(part.reshape(na, rc, nb * kp), "fa")
    top = part.transpose(1, 0, 2).reshape(rc, K)

    leaf_reach = mm("pm,mc->pc", pivot_inverse[0, 0], leaf_coupling_all).astype(BF16)
    leaf_pivots = leaf_pivot_block[0] - mm("pk,kr->pr", leaf_vectors_pivot[0, 0], leaf_y_all)
    wide = jnp.concatenate([leaf_reach, folded(leaf_pivots.astype(BF16))], axis=0)
    gathered = lax.all_gather(after(wide, y_block), FRONT, axis=0)
    leaf_reach_all = gathered[:, :kp].reshape(K, C)
    leaf_pivots_all = unfolded(gathered[:, kp:]).reshape(K, R)
    leaf_own = mm("pm,mr->pr", pivot_inverse[0, 0], leaf_pivots_all)

    pivot_ids = jnp.arange(K, dtype=jnp.int32)[:, None]
    node_pick = (pivot_ids == parent_columns[0, 1][None]).astype(BF16)
    leaf_pick = (pivot_ids == parent_columns[0, 0][None]).astype(BF16)

    def reached(parent, pick, reach):
        chosen = mm("rp,pc->rc", parent, pick).astype(BF16)
        return mm("rc,pc->rp", chosen, reach)

    node = top
    for height in range(LEVELS, 0, -1):
        if height == LEVELS:
            parent = from_behind(node, subtree // 2)
        else:
            offset = 2 ** (height - 1)
            parent = added(from_behind(node, -offset), from_behind(node, offset))
        node = (top - reached(parent, node_pick, node_reach_all)).astype(BF16)
    parent = added(from_behind(node, -1), node)
    leaf = reached(parent, leaf_pick, leaf_reach_all).astype(BF16)
    both = jnp.stack([leaf, node]).reshape(2, rc, fronts, kp).transpose(2, 0, 1, 3)
    both = exchange(both, FRONT).reshape(na, nb, 2, rc, kp)
    both = both.transpose(2, 4, 1, 0, 3).reshape(2, kp, R)
    leaf = (leaf_own - both[0]).astype(BF16)
    return (jnp.stack([leaf, both[1]])[None], remainder[None])


def solution(mesh):
    leaves, fronts = mesh.devices.shape
    nb = next(n for n in range(max(1, int(fronts**0.5)), 0, -1) if fronts % n == 0)
    grid = Mesh(mesh.devices.reshape(leaves, fronts // nb, nb), ("leaf", "fa", "fb"))
    rows3 = P("leaf", FRONT, None)
    rows4 = P("leaf", None, FRONT, None)
    in_specs = (
        *([rows3] * 4),
        *([rows4] * 4),
        P("leaf", None),
        P("leaf", None, None),
        rows4,
        rows4,
    )
    return jax.shard_map(
        per_device, mesh=grid, in_specs=in_specs, out_specs=(rows4, rows3), check_vma=False
    )
```

```python
import jax
import jax.numpy as jnp
from jax import lax
from jax.sharding import Mesh
from jax.sharding import PartitionSpec as P

LEVELS = 2
FRONT = ("fa", "fb")
BF16 = jnp.bfloat16
F32 = jnp.float32


def mm(spec, a, b):
    return jnp.einsum(spec, a, b, preferred_element_type=F32)


def from_behind(block, distance):
    count = lax.axis_size("leaf")
    return lax.ppermute(block, "leaf", [((i - distance) % count, i) for i in range(count)])


def exchange(parts, axis):
    return lax.all_to_all(parts, axis, split_axis=0, concat_axis=0, tiled=True)


def to_all(block, axis):
    count = 1
    for name in (axis,) if isinstance(axis, str) else axis:
        count *= lax.axis_size(name)
    return exchange(jnp.broadcast_to(block, (count, *block.shape)), axis)


def total(parts):
    return jnp.sum(parts.astype(F32), axis=0)


def after(block, earlier):
    corner = earlier[(0,) * (earlier.ndim - 1) + (slice(0, 1),)]
    return block + (corner * 0).astype(block.dtype)


def added(first, second):
    return (first.astype(F32) + second.astype(F32)).astype(BF16)


def folded(block):
    half = block.shape[0] // 2
    return jnp.concatenate([block[:half], block[half:]], axis=1)


def unfolded(blocks):
    half = blocks.shape[-1] // 2
    return jnp.concatenate([blocks[..., :half], blocks[..., half:]], axis=-2)


def per_device(
    leaf_pivot_block,
    leaf_rest_block,
    node_pivot_block,
    node_rest_block,
    leaf_vectors_pivot,
    leaf_vectors_rest,
    node_vectors_pivot,
    node_vectors_rest,
    stack_place,
    parent_columns,
    coupling,
    pivot_inverse,
):
    na, nb = lax.axis_size("fa"), lax.axis_size("fb")
    fronts = na * nb
    ia, ib = lax.axis_index("fa"), lax.axis_index("fb")
    me = ia * nb + ib
    kp = leaf_vectors_pivot.shape[2]
    kc = leaf_vectors_rest.shape[2]
    ks = kp + kc
    K, C = kp * fronts, kc * fronts
    R = leaf_pivot_block.shape[2]
    rc, rb = R // fronts, R // nb
    place = stack_place[0]
    subtree = 2**LEVELS

    def stack_rows(device):
        device = jnp.asarray(device, jnp.int32)
        return jnp.concatenate(
            [
                device * kp + jnp.arange(kp, dtype=jnp.int32),
                K + device * kc + jnp.arange(kc, dtype=jnp.int32),
            ]
        )

    node_w = jnp.concatenate([node_vectors_pivot[0, 1], node_vectors_rest[0, 1]], axis=0)
    node_v = jnp.concatenate([node_vectors_pivot[0, 0], node_vectors_rest[0, 0]], axis=0)
    rows = stack_rows(me)

    own_hit = rows[:, None] == place[None]
    own = jnp.concatenate([node_pivot_block[0], node_rest_block[0]], axis=0)
    own = jnp.where(jnp.any(own_hit, axis=1)[:, None], jnp.zeros_like(own), own)

    wide = jnp.concatenate([node_vectors_rest[0, 0], leaf_vectors_rest[0, 0]], axis=0)
    gathered = lax.all_gather(wide, FRONT, axis=0)
    node_ve_all = gathered[:, :kc].reshape(C, K)
    leaf_ve_all = gathered[:, kc:].reshape(C, K)

    leaf_partial = mm("ir,ik->rk", leaf_pivot_block[0], leaf_vectors_pivot[0, 1])
    leaf_partial = leaf_partial + mm("ir,ik->rk", leaf_rest_block[0], leaf_vectors_rest[0, 1])
    leaf_part = total(exchange(leaf_partial.astype(BF16).reshape(nb, rb, K), "fb")).astype(BF16)
    leaf_y = total(exchange(leaf_part.reshape(rb, na, K // na).transpose(1, 0, 2), "fa")).astype(BF16)

    both = jnp.concatenate([leaf_rest_block[0], own], axis=0).T.reshape(nb, rb, kc + ks)
    both = exchange(both, "fb")
    leaf_rest = both[:, :, :kc].transpose(1, 0, 2).reshape(rb, nb * kc)
    own_columns = both[:, :, kc:].transpose(1, 0, 2).reshape(rb, nb * ks)

    blocks = jnp.concatenate([node_w, node_v], axis=0).reshape(2 * ks, nb, K // nb).transpose(1, 0, 2)
    own_folded = folded(own)
    blocks = jnp.concatenate([blocks, jnp.broadcast_to(own_folded, (nb, *own_folded.shape))], axis=1)
    blocks = exchange(after(blocks, both), "fb")
    w_block = blocks[:, :ks].reshape(nb * ks, K // nb)
    v_block = blocks[:, ks : 2 * ks].reshape(nb * ks, K // nb)
    own_block = unfolded(blocks[:, 2 * ks :]).reshape(nb * ks, R)

    product = mm("sk,ck->sc", node_w, node_ve_all)
    unit = (rows[:, None] == K + jnp.arange(C, dtype=jnp.int32)[None]).astype(F32)
    section_rows = (after(after(unit, leaf_y), blocks) - product).astype(BF16)
    section_block = to_all(section_rows, "fb").reshape(nb * ks, C)
    block_rows = jnp.concatenate([stack_rows(ia * nb + b) for b in range(nb)])
    block_hit = (place[:, None] == block_rows[None]).astype(BF16)

    wide = jnp.concatenate([coupling[0, 1], coupling[0, 0], leaf_y], axis=0)
    gathered = lax.all_gather(after(wide, section_rows), FRONT, axis=0)
    node_coupling_all = gathered[:, :kp].reshape(K, C)
    leaf_coupling_all = gathered[:, kp : 2 * kp].reshape(K, C)
    leaf_y_all = gathered[:, 2 * kp :].reshape(na, nb, rb, K // na).transpose(1, 2, 0, 3).reshape(R, K)

    def summed(part):
        return total(to_all(part.astype(BF16), "fa")).astype(BF16)

    is_mine = jnp.arange(C, dtype=jnp.int32) // (nb * kc) == ia
    part = jnp.where(is_mine[None], jnp.tile(leaf_rest.astype(F32), (1, na)), 0.0)
    rest = summed(part - mm("rk,ck->rc", leaf_part, leaf_ve_all))
    section_map = mm("js,sc->jc", block_hit, section_block).astype(BF16)
    section_own = mm("rs,sc->rc", own_columns, section_block)

    def section(left, right):
        children = jnp.concatenate([left, right], axis=1)
        return summed(section_own + mm("rj,jc->rc", children, section_map))

    inverse_block = pivot_inverse[0, 1].reshape(kp, na, nb, kp).transpose(2, 0, 1, 3)
    inverse_block = after(inverse_block.reshape(nb, kp, na * kp), rest)
    inverse_block = exchange(inverse_block, "fb").reshape(nb * kp, na * kp)

    rest = section(after(from_behind(rest, 1), inverse_block), rest)
    rest = section(from_behind(rest, 1), from_behind(rest, -1))
    w_left = mm("cs,sk->ck", block_hit[:C], w_block).astype(BF16)
    y_own = mm("sr,sk->rk", own_block, w_block)
    left = to_all(from_behind(rest, -(subtree // 2)), "fb").reshape(R, C)

    node_reach = mm("pm,mc->pc", after(pivot_inverse[0, 1], rest), node_coupling_all).astype(BF16)
    leaf_reach = mm("pm,mc->pc", after(pivot_inverse[0, 0], rest), leaf_coupling_all).astype(BF16)
    leaf_pivots = mm("pk,rk->pr", after(leaf_vectors_pivot[0, 0], rest), leaf_y_all)
    leaf_pivots = (leaf_pivot_block[0] - leaf_pivots).astype(BF16)
    wide = jnp.concatenate([node_reach, leaf_reach, folded(leaf_pivots)], axis=0)
    gathered = lax.all_gather(wide, FRONT, axis=0)
    node_reach_all = gathered[:, :kp].reshape(K, C)
    leaf_reach_all = gathered[:, kp : 2 * kp].reshape(K, C)
    leaf_pivots_all = unfolded(gathered[:, 2 * kp :]).reshape(K, R)
    leaf_own = mm("pm,mr->pr", pivot_inverse[0, 0], leaf_pivots_all)

    partial_y = (y_own + mm("rc,ck->rk", left, w_left)).astype(BF16)
    part = total(exchange(partial_y.reshape(na, R // na, K // nb), "fa")).astype(BF16)
    y_block = to_all(part, "fa").reshape(R, K // nb)
    part = mm("sk,rk->sr", v_block, y_block).astype(BF16).reshape(nb, ks, R)
    placed = mm("sc,rc->sr", own_hit[:, :C].astype(BF16), left)
    reflected = own.astype(F32) + placed - total(exchange(part, "fb"))
    reflected = reflected.astype(BF16)
    remainder = reflected[kp:]
    pivots = to_all(reflected[:kp], "fa").reshape(na * kp, R)
    part = mm("mr,pm->rp", pivots, inverse_block).astype(BF16)
    part = total(exchange(part.reshape(nb, R // nb, nb * kp), "fb")).astype(BF16)
    part = exchange(part.reshape(na, rc, nb * kp), "fa")
    top = part.transpose(1, 0, 2).reshape(rc, K)

    pivot_ids = jnp.arange(K, dtype=jnp.int32)[:, None]
    node_pick = (pivot_ids == parent_columns[0, 1][None]).astype(BF16)
    leaf_pick = (pivot_ids == parent_columns[0, 0][None]).astype(BF16)

    def reached(parent, pick, reach):
        chosen = mm("rp,pc->rc", parent, pick).astype(BF16)
        return mm("rc,pc->rp", chosen, reach)

    node = top
    for height in range(LEVELS, 0, -1):
        if height == LEVELS:
            parent = from_behind(node, subtree // 2)
        else:
            offset = 2 ** (height - 1)
            parent = added(from_behind(node, -offset), from_behind(node, offset))
        node = (top - reached(parent, node_pick, node_reach_all)).astype(BF16)
    parent = added(from_behind(node, -1), node)
    leaf = reached(parent, leaf_pick, leaf_reach_all).astype(BF16)
    both = jnp.stack([leaf, node]).reshape(2, rc, fronts, kp).transpose(2, 0, 1, 3)
    both = exchange(both, FRONT).reshape(na, nb, 2, rc, kp)
    both = both.transpose(2, 4, 1, 0, 3).reshape(2, kp, R)
    leaf = (leaf_own - both[0]).astype(BF16)
    return (jnp.stack([leaf, both[1]])[None], remainder[None])


def solution(mesh):
    leaves, fronts = mesh.devices.shape
    nb = next(n for n in range(max(1, int(fronts**0.5)), 0, -1) if fronts % n == 0)
    grid = Mesh(mesh.devices.reshape(leaves, fronts // nb, nb), ("leaf", "fa", "fb"))
    rows3 = P("leaf", FRONT, None)
    rows4 = P("leaf", None, FRONT, None)
    in_specs = (
        *([rows3] * 4),
        *([rows4] * 4),
        P("leaf", None),
        P("leaf", None, None),
        rows4,
        rows4,
    )
    return jax.shard_map(
        per_device, mesh=grid, in_specs=in_specs, out_specs=(rows4, rows3), check_vma=False
    )
```

```python
import jax
import jax.numpy as jnp
from jax import lax
from jax.sharding import Mesh
from jax.sharding import PartitionSpec as P

LEVELS = 2
FRONT = ("fa", "fb")
BF16 = jnp.bfloat16
F32 = jnp.float32


def mm(spec, a, b):
    return jnp.einsum(spec, a, b, preferred_element_type=F32)


def from_behind(block, distance):
    count = lax.axis_size("leaf")
    return lax.ppermute(block, "leaf", [((i - distance) % count, i) for i in range(count)])


def exchange(parts, axis):
    return lax.all_to_all(parts, axis, split_axis=0, concat_axis=0, tiled=True)


def to_all(block, axis):
    count = 1
    for name in (axis,) if isinstance(axis, str) else axis:
        count *= lax.axis_size(name)
    return exchange(jnp.broadcast_to(block, (count, *block.shape)), axis)


def total(parts):
    return jnp.sum(parts.astype(F32), axis=0)


def after(block, earlier):
    corner = earlier[(0,) * (earlier.ndim - 1) + (slice(0, 1),)]
    return block + (corner * 0).astype(block.dtype)


def added(first, second):
    return (first.astype(F32) + second.astype(F32)).astype(BF16)


def folded(block):
    half = block.shape[0] // 2
    return jnp.concatenate([block[:half], block[half:]], axis=1)


def unfolded(blocks):
    half = blocks.shape[-1] // 2
    return jnp.concatenate([blocks[..., :half], blocks[..., half:]], axis=-2)


def per_device(
    leaf_pivot_block,
    leaf_rest_block,
    node_pivot_block,
    node_rest_block,
    leaf_vectors_pivot,
    leaf_vectors_rest,
    node_vectors_pivot,
    node_vectors_rest,
    stack_place,
    parent_columns,
    coupling,
    pivot_inverse,
):
    na, nb = lax.axis_size("fa"), lax.axis_size("fb")
    fronts = na * nb
    ia, ib = lax.axis_index("fa"), lax.axis_index("fb")
    me = ia * nb + ib
    kp = leaf_vectors_pivot.shape[2]
    kc = leaf_vectors_rest.shape[2]
    ks = kp + kc
    K, C = kp * fronts, kc * fronts
    R = leaf_pivot_block.shape[2]
    rc, rb = R // fronts, R // nb
    place = stack_place[0]
    subtree = 2**LEVELS

    def stack_rows(device):
        device = jnp.asarray(device, jnp.int32)
        return jnp.concatenate(
            [
                device * kp + jnp.arange(kp, dtype=jnp.int32),
                K + device * kc + jnp.arange(kc, dtype=jnp.int32),
            ]
        )

    node_w = jnp.concatenate([node_vectors_pivot[0, 1], node_vectors_rest[0, 1]], axis=0)
    node_v = jnp.concatenate([node_vectors_pivot[0, 0], node_vectors_rest[0, 0]], axis=0)
    rows = stack_rows(me)

    own_hit = rows[:, None] == place[None]
    own = jnp.concatenate([node_pivot_block[0], node_rest_block[0]], axis=0)
    own = jnp.where(jnp.any(own_hit, axis=1)[:, None], jnp.zeros_like(own), own)

    wide = jnp.concatenate([node_vectors_rest[0, 0], leaf_vectors_rest[0, 0]], axis=0)
    gathered = lax.all_gather(wide, FRONT, axis=0)
    node_ve_all = gathered[:, :kc].reshape(C, K)
    leaf_ve_all = gathered[:, kc:].reshape(C, K)

    leaf_partial = mm("ir,ik->rk", leaf_pivot_block[0], leaf_vectors_pivot[0, 1])
    leaf_partial = leaf_partial + mm("ir,ik->rk", leaf_rest_block[0], leaf_vectors_rest[0, 1])
    leaf_part = total(exchange(leaf_partial.astype(BF16).reshape(nb, rb, K), "fb")).astype(BF16)

    both = jnp.concatenate([leaf_rest_block[0], own], axis=0).T.reshape(nb, rb, kc + ks)
    both = exchange(both, "fb")
    leaf_rest = both[:, :, :kc].transpose(1, 0, 2).reshape(rb, nb * kc)
    own_columns = both[:, :, kc:].transpose(1, 0, 2).reshape(rb, nb * ks)

    blocks = jnp.concatenate([node_w, node_v], axis=0).reshape(2 * ks, nb, K // nb).transpose(1, 0, 2)
    own_folded = folded(own)
    blocks = jnp.concatenate([blocks, jnp.broadcast_to(own_folded, (nb, *own_folded.shape))], axis=1)
    blocks = exchange(after(after(blocks, both), leaf_part), "fb")
    w_block = blocks[:, :ks].reshape(nb * ks, K // nb)
    v_block = blocks[:, ks : 2 * ks].reshape(nb * ks, K // nb)
    own_block = unfolded(blocks[:, 2 * ks :]).reshape(nb * ks, R)

    inverse_block = pivot_inverse[0, 1].reshape(kp, na, nb, kp).transpose(2, 0, 1, 3)
    inverse_block = after(inverse_block.reshape(nb, kp, na * kp), blocks)
    inverse_block = exchange(inverse_block, "fb").reshape(nb * kp, na * kp)

    product = mm("sk,ck->sc", node_w, node_ve_all)
    unit = (rows[:, None] == K + jnp.arange(C, dtype=jnp.int32)[None]).astype(F32)
    section_rows = (after(unit, inverse_block) - product).astype(BF16)
    section_block = to_all(section_rows, "fb").reshape(nb * ks, C)
    block_rows = jnp.concatenate([stack_rows(ia * nb + b) for b in range(nb)])
    block_hit = (place[:, None] == block_rows[None]).astype(BF16)

    def summed(part):
        return total(to_all(part.astype(BF16), "fa")).astype(BF16)

    is_mine = jnp.arange(C, dtype=jnp.int32) // (nb * kc) == ia
    part = jnp.where(is_mine[None], jnp.tile(leaf_rest.astype(F32), (1, na)), 0.0)
    rest = summed(part - mm("rk,ck->rc", leaf_part, leaf_ve_all))
    leaf_y = after(leaf_part, section_rows).reshape(rb, na, K // na).transpose(1, 0, 2)
    leaf_y = lax.psum_scatter(leaf_y, "fa", scatter_dimension=0)
    wide = jnp.concatenate([coupling[0, 1], coupling[0, 0], leaf_y], axis=0)
    gathered = lax.all_gather(after(after(wide, rest), section_block), FRONT, axis=0)
    node_coupling_all = gathered[:, :kp].reshape(K, C)
    leaf_coupling_all = gathered[:, kp : 2 * kp].reshape(K, C)
    leaf_y_all = gathered[:, 2 * kp :].reshape(na, nb, rb, K // na).transpose(1, 2, 0, 3).reshape(R, K)

    section_map = mm("js,sc->jc", block_hit, section_block).astype(BF16)
    section_own = mm("rs,sc->rc", own_columns, section_block)

    def section(left, right):
        children = jnp.concatenate([left, right], axis=1)
        return summed(section_own + mm("rj,jc->rc", children, section_map))

    rest = section(from_behind(rest, 1), rest)
    rest = section(from_behind(rest, 1), from_behind(rest, -1))
    w_left = mm("cs,sk->ck", block_hit[:C], w_block).astype(BF16)
    y_own = mm("sr,sk->rk", own_block, w_block)
    left = to_all(from_behind(rest, -(subtree // 2)), "fb").reshape(R, C)

    partial_y = (y_own + mm("rc,ck->rk", left, w_left)).astype(BF16)
    part = total(exchange(partial_y.reshape(na, R // na, K // nb), "fa")).astype(BF16)
    node_reach = mm("pm,mc->pc", after(pivot_inverse[0, 1], part), node_coupling_all).astype(BF16)
    leaf_reach = mm("pm,mc->pc", after(pivot_inverse[0, 0], part), leaf_coupling_all).astype(BF16)
    leaf_pivots = mm("pk,rk->pr", after(leaf_vectors_pivot[0, 0], part), leaf_y_all)
    leaf_pivots = (leaf_pivot_block[0] - leaf_pivots).astype(BF16)
    wide = jnp.concatenate([node_reach, leaf_reach, folded(leaf_pivots)], axis=0)
    gathered = lax.all_gather(wide, FRONT, axis=0)
    node_reach_all = gathered[:, :kp].reshape(K, C)
    leaf_reach_all = gathered[:, kp : 2 * kp].reshape(K, C)
    leaf_pivots_all = unfolded(gathered[:, 2 * kp :]).reshape(K, R)
    leaf_own = mm("pm,mr->pr", pivot_inverse[0, 0], leaf_pivots_all)

    y_block = to_all(part, "fa").reshape(R, K // nb)
    part = mm("sk,rk->sr", v_block, y_block).astype(BF16).reshape(nb, ks, R)
    placed = mm("sc,rc->sr", own_hit[:, :C].astype(BF16), left)
    reflected = own.astype(F32) + placed - total(exchange(part, "fb"))
    reflected = reflected.astype(BF16)
    remainder = reflected[kp:]
    pivots = to_all(reflected[:kp], "fa").reshape(na * kp, R)
    part = mm("mr,pm->rp", pivots, inverse_block).astype(BF16)
    part = total(exchange(part.reshape(nb, R // nb, nb * kp), "fb")).astype(BF16)
    part = exchange(part.reshape(na, rc, nb * kp), "fa")
    top = part.transpose(1, 0, 2).reshape(rc, K)

    pivot_ids = jnp.arange(K, dtype=jnp.int32)[:, None]
    node_pick = (pivot_ids == parent_columns[0, 1][None]).astype(BF16)
    leaf_pick = (pivot_ids == parent_columns[0, 0][None]).astype(BF16)

    def reached(parent, pick, reach):
        chosen = mm("rp,pc->rc", parent, pick).astype(BF16)
        return mm("rc,pc->rp", chosen, reach)

    node = top
    for height in range(LEVELS, 0, -1):
        if height == LEVELS:
            parent = from_behind(node, subtree // 2)
        else:
            offset = 2 ** (height - 1)
            parent = added(from_behind(node, -offset), from_behind(node, offset))
        node = (top - reached(parent, node_pick, node_reach_all)).astype(BF16)
    parent = added(from_behind(node, -1), node)
    leaf = reached(parent, leaf_pick, leaf_reach_all).astype(BF16)
    both = jnp.stack([leaf, node]).reshape(2, rc, fronts, kp).transpose(2, 0, 1, 3)
    both = exchange(both, FRONT).reshape(na, nb, 2, rc, kp)
    both = both.transpose(2, 4, 1, 0, 3).reshape(2, kp, R)
    leaf = (leaf_own - both[0]).astype(BF16)
    return (jnp.stack([leaf, both[1]])[None], remainder[None])


def solution(mesh):
    leaves, fronts = mesh.devices.shape
    nb = next(n for n in range(max(1, int(fronts**0.5)), 0, -1) if fronts % n == 0)
    grid = Mesh(mesh.devices.reshape(leaves, fronts // nb, nb), ("leaf", "fa", "fb"))
    rows3 = P("leaf", FRONT, None)
    rows4 = P("leaf", None, FRONT, None)
    in_specs = (
        *([rows3] * 4),
        *([rows4] * 4),
        P("leaf", None),
        P("leaf", None, None),
        rows4,
        rows4,
    )
    return jax.shard_map(
        per_device, mesh=grid, in_specs=in_specs, out_specs=(rows4, rows3), check_vma=False
    )
```

```python
import jax
import jax.numpy as jnp
from jax import lax
from jax.sharding import Mesh
from jax.sharding import PartitionSpec as P

LEVELS = 2
FRONT = ("fa", "fb")
BF16 = jnp.bfloat16
F32 = jnp.float32


def mm(spec, a, b):
    return jnp.einsum(spec, a, b, preferred_element_type=F32)


def from_behind(block, distance):
    count = lax.axis_size("leaf")
    return lax.ppermute(block, "leaf", [((i - distance) % count, i) for i in range(count)])


def exchange(parts, axis):
    return lax.all_to_all(parts, axis, split_axis=0, concat_axis=0, tiled=True)


def to_all(block, axis):
    count = 1
    for name in (axis,) if isinstance(axis, str) else axis:
        count *= lax.axis_size(name)
    return exchange(jnp.broadcast_to(block, (count, *block.shape)), axis)


def total(parts):
    return jnp.sum(parts.astype(F32), axis=0)


def after(block, earlier):
    corner = earlier[(0,) * (earlier.ndim - 1) + (slice(0, 1),)]
    return block + (corner * 0).astype(block.dtype)


def added(first, second):
    return (first.astype(F32) + second.astype(F32)).astype(BF16)


def folded(block):
    half = block.shape[0] // 2
    return jnp.concatenate([block[:half], block[half:]], axis=1)


def unfolded(blocks):
    half = blocks.shape[-1] // 2
    return jnp.concatenate([blocks[..., :half], blocks[..., half:]], axis=-2)


def per_device(
    leaf_pivot_block,
    leaf_rest_block,
    node_pivot_block,
    node_rest_block,
    leaf_vectors_pivot,
    leaf_vectors_rest,
    node_vectors_pivot,
    node_vectors_rest,
    stack_place,
    parent_columns,
    coupling,
    pivot_inverse,
):
    na, nb = lax.axis_size("fa"), lax.axis_size("fb")
    fronts = na * nb
    ia, ib = lax.axis_index("fa"), lax.axis_index("fb")
    me = ia * nb + ib
    kp = leaf_vectors_pivot.shape[2]
    kc = leaf_vectors_rest.shape[2]
    ks = kp + kc
    K, C = kp * fronts, kc * fronts
    R = leaf_pivot_block.shape[2]
    rc = R // fronts
    place = stack_place[0]
    subtree = 2**LEVELS

    def stack_rows(device):
        device = jnp.asarray(device, jnp.int32)
        return jnp.concatenate(
            [
                device * kp + jnp.arange(kp, dtype=jnp.int32),
                K + device * kc + jnp.arange(kc, dtype=jnp.int32),
            ]
        )

    node_w = jnp.concatenate([node_vectors_pivot[0, 1], node_vectors_rest[0, 1]], axis=0)
    node_v = jnp.concatenate([node_vectors_pivot[0, 0], node_vectors_rest[0, 0]], axis=0)
    rows = stack_rows(me)

    own_hit = rows[:, None] == place[None]
    own = jnp.concatenate([node_pivot_block[0], node_rest_block[0]], axis=0)
    own = jnp.where(jnp.any(own_hit, axis=1)[:, None], jnp.zeros_like(own), own)

    node_ve_all = lax.all_gather(node_vectors_rest[0, 0], FRONT, axis=0, tiled=True)

    leaf_partial = mm("ik,ir->kr", leaf_vectors_pivot[0, 1], leaf_pivot_block[0])
    leaf_partial = leaf_partial + mm("ik,ir->kr", leaf_vectors_rest[0, 1], leaf_rest_block[0])
    part = exchange(leaf_partial.astype(BF16).reshape(nb, K // nb, R), "fb")
    part = exchange(total(part).astype(BF16).reshape(na, kp, R), "fa")
    leaf_y = total(part).astype(BF16)

    both = jnp.concatenate([leaf_rest_block[0], own], axis=0).T.reshape(nb, na, rc, kc + ks)
    leaf_ve = leaf_vectors_rest[0, 0].reshape(kc // rc, rc, nb, na, kp).transpose(2, 3, 1, 0, 4)
    leaf_ve = leaf_ve.reshape(nb, na, rc, kc // rc * kp)
    both = jnp.concatenate([both, leaf_ve], axis=3).transpose(1, 0, 2, 3)
    both = exchange(both.reshape(fronts, rc, both.shape[3]), FRONT)
    leaf_rest = both[:, :, :kc].transpose(1, 0, 2).reshape(rc, C)
    own_columns = both[:, :, kc : kc + ks].transpose(1, 0, 2).reshape(rc, fronts * ks)
    leaf_ve = both[:, :, kc + ks :].reshape(fronts, rc, kc // rc, kp).transpose(0, 2, 1, 3).reshape(C, kp)
    part = mm("kr,ck->rc", leaf_y, leaf_ve).astype(BF16)
    part = part.reshape(nb, na, rc, C).transpose(1, 0, 2, 3).reshape(fronts, rc, C)
    rest = (leaf_rest - total(exchange(part, FRONT))).astype(BF16)

    product = mm("sk,ck->sc", node_w, node_ve_all)
    unit = (rows[:, None] == K + jnp.arange(C, dtype=jnp.int32)[None]).astype(F32)
    section_rows = (after(unit, leaf_y) - product).astype(BF16)

    section_all = lax.all_gather(section_rows, FRONT, axis=0, tiled=True)

    blocks = node_w.reshape(ks, nb, K // nb).transpose(1, 0, 2)
    own_folded = folded(own)
    blocks = jnp.concatenate([blocks, jnp.broadcast_to(own_folded, (nb, *own_folded.shape))], axis=1)
    blocks = exchange(after(blocks, rest), "fb")
    w_block = blocks[:, :ks].reshape(nb * ks, K // nb)
    own_block = unfolded(blocks[:, ks:]).reshape(nb * ks, R)
    v_parts = after(node_v, rest).reshape(ks, nb, K // nb).transpose(1, 0, 2)
    v_parts = [lax.dynamic_index_in_dim(v_parts, (ib + d) % nb, keepdims=False) for d in range(nb)]
    v_parts = [
        lax.ppermute(part, "fb", [(i, (i + d) % nb) for i in range(nb)]) if d else part
        for d, part in enumerate(v_parts)
    ]
    v_parts = jnp.stack([v_parts[-d % nb] for d in range(nb)])

    inverse_block = pivot_inverse[0, 1].reshape(kp, na, nb, kp).transpose(2, 0, 1, 3)
    inverse_block = exchange(inverse_block.reshape(nb, kp, na * kp), "fb")
    inverse_block = inverse_block.reshape(nb * kp, na * kp)
    block_rows = jnp.concatenate([stack_rows(ia * nb + b) for b in range(nb)])
    block_hit = (place[:C, None] == block_rows[None]).astype(BF16)
    v_block = lax.dynamic_slice_in_dim(jnp.concatenate([v_parts, v_parts]), (nb - ib) % nb, nb)
    w_left = mm("cs,sk->ck", block_hit, w_block).astype(BF16)
    y_own = mm("sr,sk->rk", own_block, w_block)

    rest = after(rest, inverse_block)
    wide = jnp.concatenate([coupling[0, 1], folded(leaf_y)], axis=0)
    gathered = lax.all_gather(after(wide, rest), FRONT, axis=0)
    node_coupling_all = gathered[:, :kp].reshape(K, C)
    leaf_y_all = unfolded(gathered[:, kp:]).reshape(na, nb, kp, R).transpose(1, 0, 2, 3).reshape(K, R)

    device = jnp.where(place < K, place // kp, (place - K) // kc)
    within = jnp.where(place < K, place % kp, kp + (place - K) % kc)
    section_map = jnp.take(section_all, after(device * ks + within, rest[0]), axis=0)
    section_own = mm("rs,sc->rc", after(own_columns, rest), section_all)

    def section(left, right):
        children = jnp.concatenate([left, right], axis=1)
        return (section_own + mm("rj,jc->rc", children, section_map)).astype(BF16)

    rest = section(from_behind(rest, 1), rest)
    rest = section(from_behind(rest, 1), from_behind(rest, -1))
    left = to_all(from_behind(rest, -(subtree // 2)), FRONT)
    left = left.reshape(na, nb, rc, C).transpose(1, 0, 2, 3).reshape(R, C)

    partial_y = (after(y_own, v_block) + mm("rc,ck->rk", left, w_left)).astype(BF16)
    part = total(exchange(partial_y.reshape(na, R // na, K // nb), "fa")).astype(BF16)
    node_reach = mm("pm,mc->pc", after(pivot_inverse[0, 1], part), node_coupling_all).astype(BF16)
    leaf_pivots = mm("pk,kr->pr", after(leaf_vectors_pivot[0, 0], part), leaf_y_all)
    leaf_pivots = (leaf_pivot_block[0] - leaf_pivots).astype(BF16)
    wide = jnp.concatenate([node_reach, coupling[0, 0], folded(leaf_pivots)], axis=0)
    gathered = lax.all_gather(wide, FRONT, axis=0)
    node_reach_all = gathered[:, :kp].reshape(K, C)
    leaf_coupling_all = gathered[:, kp : 2 * kp].reshape(K, C)
    leaf_pivots_all = unfolded(gathered[:, 2 * kp :]).reshape(K, R)
    leaf_reach = mm("pm,mc->pc", pivot_inverse[0, 0], leaf_coupling_all).astype(BF16)
    leaf_own = mm("pm,mr->pr", pivot_inverse[0, 0], leaf_pivots_all)

    y_block = to_all(part, "fa").reshape(R, K // nb)
    part = mm("bsk,rk->bsr", v_block, y_block).astype(BF16)
    placed = mm("sc,rc->sr", own_hit[:, :C].astype(BF16), left)
    reflected = own.astype(F32) + placed - total(exchange(part, "fb"))
    reflected = reflected.astype(BF16)
    remainder = reflected[kp:]
    pivots = to_all(reflected[:kp], "fa").reshape(na * kp, R)
    part = mm("mr,pm->rp", pivots, inverse_block).astype(BF16)
    part = total(exchange(part.reshape(nb, R // nb, nb * kp), "fb")).astype(BF16)
    part = exchange(part.reshape(na, rc, nb * kp), "fa")
    top = part.transpose(1, 0, 2).reshape(rc, K)

    pivot_ids = jnp.arange(K, dtype=jnp.int32)[:, None]
    node_pick = (pivot_ids == parent_columns[0, 1][None]).astype(BF16)
    leaf_pick = (pivot_ids == parent_columns[0, 0][None]).astype(BF16)

    def chosen(parent, pick):
        return mm("rp,pc->rc", parent, pick).astype(BF16)

    node = top
    for height in range(LEVELS, 0, -1):
        if height == LEVELS:
            parent = from_behind(node, subtree // 2)
        else:
            offset = 2 ** (height - 1)
            parent = added(from_behind(node, -offset), from_behind(node, offset))
        node = (top - mm("rc,pc->rp", chosen(parent, node_pick), node_reach_all)).astype(BF16)
    parent = chosen(added(from_behind(node, -1), node), leaf_pick)
    both = node.reshape(rc, fronts, kp).transpose(1, 0, 2)
    both = jnp.concatenate([both, jnp.broadcast_to(parent, (fronts, rc, C))], axis=2)
    both = exchange(both, FRONT).reshape(na, nb, rc, kp + C).transpose(1, 0, 2, 3).reshape(R, kp + C)
    leaf = (leaf_own - mm("pc,rc->pr", leaf_reach, both[:, kp:])).astype(BF16)
    return (jnp.stack([leaf, both[:, :kp].T])[None], remainder[None])


def solution(mesh):
    leaves, fronts = mesh.devices.shape
    nb = next(n for n in range(max(1, int(fronts**0.5)), 0, -1) if fronts % n == 0)
    grid = Mesh(mesh.devices.reshape(leaves, fronts // nb, nb), ("leaf", "fa", "fb"))
    rows3 = P("leaf", FRONT, None)
    rows4 = P("leaf", None, FRONT, None)
    in_specs = (
        *([rows3] * 4),
        *([rows4] * 4),
        P("leaf", None),
        P("leaf", None, None),
        rows4,
        rows4,
    )
    return jax.shard_map(
        per_device, mesh=grid, in_specs=in_specs, out_specs=(rows4, rows3), check_vma=False
    )
```

```python
import jax
import jax.numpy as jnp
from jax import lax
from jax.sharding import Mesh
from jax.sharding import PartitionSpec as P

LEVELS = 2
FRONT = ("fa", "fb")
BF16 = jnp.bfloat16
F32 = jnp.float32


def mm(spec, a, b):
    return jnp.einsum(spec, a, b, preferred_element_type=F32)


def from_behind(block, distance):
    count = lax.axis_size("leaf")
    return lax.ppermute(block, "leaf", [((i - distance) % count, i) for i in range(count)])


def exchange(parts, axis):
    return lax.all_to_all(parts, axis, split_axis=0, concat_axis=0, tiled=True)


def to_all(block, axis):
    count = 1
    for name in (axis,) if isinstance(axis, str) else axis:
        count *= lax.axis_size(name)
    return exchange(jnp.broadcast_to(block, (count, *block.shape)), axis)


def total(parts):
    return jnp.sum(parts.astype(F32), axis=0)


def after(block, earlier):
    corner = earlier[(0,) * (earlier.ndim - 1) + (slice(0, 1),)]
    return block + (corner * 0).astype(block.dtype)


def added(first, second):
    return (first.astype(F32) + second.astype(F32)).astype(BF16)


def folded(block):
    half = block.shape[0] // 2
    return jnp.concatenate([block[:half], block[half:]], axis=1)


def unfolded(blocks):
    half = blocks.shape[-1] // 2
    return jnp.concatenate([blocks[..., :half], blocks[..., half:]], axis=-2)


def per_device(
    leaf_pivot_block,
    leaf_rest_block,
    node_pivot_block,
    node_rest_block,
    leaf_vectors_pivot,
    leaf_vectors_rest,
    node_vectors_pivot,
    node_vectors_rest,
    stack_place,
    parent_columns,
    coupling,
    pivot_inverse,
):
    na, nb = lax.axis_size("fa"), lax.axis_size("fb")
    fronts = na * nb
    ia, ib = lax.axis_index("fa"), lax.axis_index("fb")
    me = ia * nb + ib
    kp = leaf_vectors_pivot.shape[2]
    kc = leaf_vectors_rest.shape[2]
    ks = kp + kc
    K, C = kp * fronts, kc * fronts
    R = leaf_pivot_block.shape[2]
    rc = R // fronts
    place = stack_place[0]
    subtree = 2**LEVELS

    def stack_rows(device):
        device = jnp.asarray(device, jnp.int32)
        return jnp.concatenate(
            [
                device * kp + jnp.arange(kp, dtype=jnp.int32),
                K + device * kc + jnp.arange(kc, dtype=jnp.int32),
            ]
        )

    node_w = jnp.concatenate([node_vectors_pivot[0, 1], node_vectors_rest[0, 1]], axis=0)
    node_v = jnp.concatenate([node_vectors_pivot[0, 0], node_vectors_rest[0, 0]], axis=0)
    rows = stack_rows(me)

    own_hit = rows[:, None] == place[None]
    own = jnp.concatenate([node_pivot_block[0], node_rest_block[0]], axis=0)
    own = jnp.where(jnp.any(own_hit, axis=1)[:, None], jnp.zeros_like(own), own)

    node_ve_all = lax.all_gather(node_vectors_rest[0, 0], FRONT, axis=0, tiled=True)

    leaf_partial = mm("ik,ir->kr", leaf_vectors_pivot[0, 1], leaf_pivot_block[0])
    leaf_partial = leaf_partial + mm("ik,ir->kr", leaf_vectors_rest[0, 1], leaf_rest_block[0])
    part = exchange(leaf_partial.astype(BF16).reshape(nb, K // nb, R), "fb")
    part = exchange(total(part).astype(BF16).reshape(na, kp, R), "fa")
    leaf_y = total(part).astype(BF16)

    both = jnp.concatenate([leaf_rest_block[0], own], axis=0).T.reshape(nb, na, rc, kc + ks)
    leaf_ve = leaf_vectors_rest[0, 0].reshape(kc // rc, rc, nb, na, kp).transpose(2, 3, 1, 0, 4)
    leaf_ve = leaf_ve.reshape(nb, na, rc, kc // rc * kp)
    both = jnp.concatenate([both, leaf_ve], axis=3).transpose(1, 0, 2, 3)
    both = exchange(both.reshape(fronts, rc, both.shape[3]), FRONT)
    leaf_rest = both[:, :, :kc].transpose(1, 0, 2).reshape(rc, C)
    own_columns = both[:, :, kc : kc + ks].transpose(1, 0, 2).reshape(rc, fronts * ks)
    leaf_ve = both[:, :, kc + ks :].reshape(fronts, rc, kc // rc, kp).transpose(0, 2, 1, 3).reshape(C, kp)
    part = mm("kr,ck->rc", leaf_y, leaf_ve).astype(BF16)
    part = part.reshape(nb, na, rc, C).transpose(1, 0, 2, 3).reshape(fronts, rc, C)
    rest = (leaf_rest - total(exchange(part, FRONT))).astype(BF16)

    product = mm("sk,ck->sc", node_w, node_ve_all)
    unit = (rows[:, None] == K + jnp.arange(C, dtype=jnp.int32)[None]).astype(F32)
    section_rows = (after(unit, leaf_y) - product).astype(BF16)

    section_all = lax.all_gather(section_rows, FRONT, axis=0, tiled=True)

    blocks = jnp.concatenate([node_w, node_v], axis=0).reshape(2 * ks, nb, K // nb).transpose(1, 0, 2)
    own_folded = folded(own)
    blocks = jnp.concatenate([blocks, jnp.broadcast_to(own_folded, (nb, *own_folded.shape))], axis=1)
    blocks = exchange(after(blocks, rest), "fb")
    w_block = blocks[:, :ks].reshape(nb * ks, K // nb)
    v_block = blocks[:, ks : 2 * ks]
    own_block = unfolded(blocks[:, 2 * ks :]).reshape(nb * ks, R)

    inverse_block = pivot_inverse[0, 1].reshape(kp, na, nb, kp).transpose(2, 0, 1, 3)
    inverse_block = exchange(inverse_block.reshape(nb, kp, na * kp), "fb")
    inverse_block = inverse_block.reshape(nb * kp, na * kp)
    block_rows = jnp.concatenate([stack_rows(ia * nb + b) for b in range(nb)])
    block_hit = (place[:C, None] == block_rows[None]).astype(BF16)
    w_left = mm("cs,sk->ck", block_hit, w_block).astype(BF16)
    y_own = mm("sr,sk->rk", own_block, w_block)

    rest = after(rest, inverse_block)
    wide = jnp.concatenate([coupling[0, 1], coupling[0, 0], folded(leaf_y)], axis=0)
    gathered = lax.all_gather(after(wide, rest), FRONT, axis=0)
    node_coupling_all = gathered[:, :kp].reshape(K, C)
    leaf_coupling_all = gathered[:, kp : 2 * kp].reshape(K, C)
    leaf_y_all = unfolded(gathered[:, 2 * kp :]).reshape(na, nb, kp, R).transpose(1, 0, 2, 3).reshape(K, R)

    device = jnp.where(place < K, place // kp, (place - K) // kc)
    within = jnp.where(place < K, place % kp, kp + (place - K) % kc)
    section_map = jnp.take(section_all, after(device * ks + within, rest[0]), axis=0)
    section_own = mm("rs,sc->rc", after(own_columns, rest), section_all)

    def section(left, right):
        children = jnp.concatenate([left, right], axis=1)
        return (section_own + mm("rj,jc->rc", children, section_map)).astype(BF16)

    rest = section(from_behind(rest, 1), rest)
    rest = section(from_behind(rest, 1), from_behind(rest, -1))
    left = to_all(from_behind(rest, -(subtree // 2)), FRONT)
    left = left.reshape(na, nb, rc, C).transpose(1, 0, 2, 3).reshape(R, C)

    partial_y = (y_own + mm("rc,ck->rk", left, w_left)).astype(BF16)
    part = total(exchange(partial_y.reshape(na, R // na, K // nb), "fa")).astype(BF16)
    node_reach = mm("pm,mc->pc", after(pivot_inverse[0, 1], part), node_coupling_all).astype(BF16)
    leaf_pivots = mm("pk,kr->pr", after(leaf_vectors_pivot[0, 0], part), leaf_y_all)
    leaf_pivots = (leaf_pivot_block[0] - leaf_pivots).astype(BF16)
    wide = jnp.concatenate([node_reach, folded(leaf_pivots)], axis=0)
    gathered = lax.all_gather(wide, FRONT, axis=0)
    node_reach_all = gathered[:, :kp].reshape(K, C)
    leaf_pivots_all = unfolded(gathered[:, kp:]).reshape(K, R)
    leaf_reach = mm("pm,mc->pc", pivot_inverse[0, 0], leaf_coupling_all).astype(BF16)
    leaf_own = mm("pm,mr->pr", pivot_inverse[0, 0], leaf_pivots_all)

    y_block = to_all(part, "fa").reshape(R, K // nb)
    part = mm("bsk,rk->bsr", v_block, y_block).astype(BF16)
    placed = mm("sc,rc->sr", own_hit[:, :C].astype(BF16), left)
    reflected = own.astype(F32) + placed - total(exchange(part, "fb"))
    reflected = reflected.astype(BF16)
    remainder = reflected[kp:]
    pivots = to_all(reflected[:kp], "fa").reshape(na * kp, R)
    part = mm("mr,pm->rp", pivots, inverse_block).astype(BF16)
    part = total(exchange(part.reshape(nb, R // nb, nb * kp), "fb")).astype(BF16)
    part = exchange(part.reshape(na, rc, nb * kp), "fa")
    top = part.transpose(1, 0, 2).reshape(rc, K)

    pivot_ids = jnp.arange(K, dtype=jnp.int32)[:, None]
    node_pick = (pivot_ids == parent_columns[0, 1][None]).astype(BF16)
    leaf_pick = (pivot_ids == parent_columns[0, 0][None]).astype(BF16)

    def chosen(parent, pick):
        return mm("rp,pc->rc", parent, pick).astype(BF16)

    node = top
    for height in range(LEVELS, 0, -1):
        if height == LEVELS:
            parent = from_behind(node, subtree // 2)
        else:
            offset = 2 ** (height - 1)
            parent = added(from_behind(node, -offset), from_behind(node, offset))
        node = (top - mm("rc,pc->rp", chosen(parent, node_pick), node_reach_all)).astype(BF16)
    parent = chosen(added(from_behind(node, -1), node), leaf_pick)
    both = node.reshape(rc, fronts, kp).transpose(1, 0, 2)
    both = jnp.concatenate([both, jnp.broadcast_to(parent, (fronts, rc, C))], axis=2)
    both = exchange(both, FRONT).reshape(na, nb, rc, kp + C).transpose(1, 0, 2, 3).reshape(R, kp + C)
    leaf = (leaf_own - mm("pc,rc->pr", leaf_reach, both[:, kp:])).astype(BF16)
    return (jnp.stack([leaf, both[:, :kp].T])[None], remainder[None])


def solution(mesh):
    leaves, fronts = mesh.devices.shape
    nb = next(n for n in range(max(1, int(fronts**0.5)), 0, -1) if fronts % n == 0)
    grid = Mesh(mesh.devices.reshape(leaves, fronts // nb, nb), ("leaf", "fa", "fb"))
    rows3 = P("leaf", FRONT, None)
    rows4 = P("leaf", None, FRONT, None)
    in_specs = (
        *([rows3] * 4),
        *([rows4] * 4),
        P("leaf", None),
        P("leaf", None, None),
        rows4,
        rows4,
    )
    return jax.shard_map(
        per_device, mesh=grid, in_specs=in_specs, out_specs=(rows4, rows3), check_vma=False
    )
```

```python
import jax
import jax.numpy as jnp
from jax import lax
from jax.sharding import Mesh
from jax.sharding import PartitionSpec as P

LEVELS = 2
FRONT = ("fa", "fb")
BF16 = jnp.bfloat16
F32 = jnp.float32


def mm(spec, a, b):
    return jnp.einsum(spec, a, b, preferred_element_type=F32)


def from_behind(block, distance):
    count = lax.axis_size("leaf")
    return lax.ppermute(block, "leaf", [((i - distance) % count, i) for i in range(count)])


def exchange(parts, axis):
    return lax.all_to_all(parts, axis, split_axis=0, concat_axis=0, tiled=True)


def to_all(block, axis):
    count = 1
    for name in (axis,) if isinstance(axis, str) else axis:
        count *= lax.axis_size(name)
    return exchange(jnp.broadcast_to(block, (count, *block.shape)), axis)


def total(parts):
    return jnp.sum(parts.astype(F32), axis=0)


def after(block, earlier):
    corner = earlier[(0,) * (earlier.ndim - 1) + (slice(0, 1),)]
    return block + (corner * 0).astype(block.dtype)


def added(first, second):
    return (first.astype(F32) + second.astype(F32)).astype(BF16)


def folded(block):
    half = block.shape[0] // 2
    return jnp.concatenate([block[:half], block[half:]], axis=1)


def unfolded(blocks):
    half = blocks.shape[-1] // 2
    return jnp.concatenate([blocks[..., :half], blocks[..., half:]], axis=-2)


def per_device(
    leaf_pivot_block,
    leaf_rest_block,
    node_pivot_block,
    node_rest_block,
    leaf_vectors_pivot,
    leaf_vectors_rest,
    node_vectors_pivot,
    node_vectors_rest,
    stack_place,
    parent_columns,
    coupling,
    pivot_inverse,
):
    na, nb = lax.axis_size("fa"), lax.axis_size("fb")
    fronts = na * nb
    ia, ib = lax.axis_index("fa"), lax.axis_index("fb")
    me = ia * nb + ib
    kp = leaf_vectors_pivot.shape[2]
    kc = leaf_vectors_rest.shape[2]
    ks = kp + kc
    K, C = kp * fronts, kc * fronts
    R = leaf_pivot_block.shape[2]
    rc = R // fronts
    place = stack_place[0]
    subtree = 2**LEVELS

    def stack_rows(device):
        device = jnp.asarray(device, jnp.int32)
        return jnp.concatenate(
            [
                device * kp + jnp.arange(kp, dtype=jnp.int32),
                K + device * kc + jnp.arange(kc, dtype=jnp.int32),
            ]
        )

    node_w = jnp.concatenate([node_vectors_pivot[0, 1], node_vectors_rest[0, 1]], axis=0)
    node_v = jnp.concatenate([node_vectors_pivot[0, 0], node_vectors_rest[0, 0]], axis=0)
    rows = stack_rows(me)

    own_hit = rows[:, None] == place[None]
    own = jnp.concatenate([node_pivot_block[0], node_rest_block[0]], axis=0)
    own = jnp.where(jnp.any(own_hit, axis=1)[:, None], jnp.zeros_like(own), own)

    node_ve_all = lax.all_gather(node_vectors_rest[0, 0], FRONT, axis=0, tiled=True)

    leaf_partial = mm("ik,ir->kr", leaf_vectors_pivot[0, 1], leaf_pivot_block[0])
    leaf_partial = leaf_partial + mm("ik,ir->kr", leaf_vectors_rest[0, 1], leaf_rest_block[0])
    part = exchange(leaf_partial.astype(BF16).reshape(nb, K // nb, R), "fb")
    part = exchange(total(part).astype(BF16).reshape(na, kp, R), "fa")
    leaf_y = total(part).astype(BF16)

    both = jnp.concatenate([leaf_rest_block[0], own], axis=0).T.reshape(nb, na, rc, kc + ks)
    leaf_ve = leaf_vectors_rest[0, 0].reshape(kc // rc, rc, nb, na, kp).transpose(2, 3, 1, 0, 4)
    leaf_ve = leaf_ve.reshape(nb, na, rc, kc // rc * kp)
    both = jnp.concatenate([both, leaf_ve], axis=3).transpose(1, 0, 2, 3)
    both = exchange(both.reshape(fronts, rc, both.shape[3]), FRONT)
    leaf_rest = both[:, :, :kc].transpose(1, 0, 2).reshape(rc, C)
    own_columns = both[:, :, kc : kc + ks].transpose(1, 0, 2).reshape(rc, fronts * ks)
    leaf_ve = both[:, :, kc + ks :].reshape(fronts, rc, kc // rc, kp).transpose(0, 2, 1, 3).reshape(C, kp)
    part = mm("kr,ck->rc", leaf_y, leaf_ve).astype(BF16)
    part = part.reshape(nb, na, rc, C).transpose(1, 0, 2, 3).reshape(fronts, rc, C)
    rest = (leaf_rest - total(exchange(part, FRONT))).astype(BF16)

    product = mm("sk,ck->sc", node_w, node_ve_all)
    unit = (rows[:, None] == K + jnp.arange(C, dtype=jnp.int32)[None]).astype(F32)
    section_rows = (after(unit, leaf_y) - product).astype(BF16)

    section_all = lax.all_gather(section_rows, FRONT, axis=0, tiled=True)

    blocks = jnp.concatenate([node_w, node_v], axis=0).reshape(2 * ks, nb, K // nb).transpose(1, 0, 2)
    own_folded = folded(own)
    blocks = jnp.concatenate([blocks, jnp.broadcast_to(own_folded, (nb, *own_folded.shape))], axis=1)
    blocks = exchange(after(blocks, rest), "fb")
    w_block = blocks[:, :ks].reshape(nb * ks, K // nb)
    v_block = blocks[:, ks : 2 * ks]
    own_block = unfolded(blocks[:, 2 * ks :]).reshape(nb * ks, R)

    inverse_block = pivot_inverse[0, 1].reshape(kp, na, nb, kp).transpose(2, 0, 1, 3)
    inverse_block = exchange(inverse_block.reshape(nb, kp, na * kp), "fb")
    inverse_block = inverse_block.reshape(nb * kp, na * kp)
    block_rows = jnp.concatenate([stack_rows(ia * nb + b) for b in range(nb)])
    block_hit = (place[:C, None] == block_rows[None]).astype(BF16)
    w_left = mm("cs,sk->ck", block_hit, w_block).astype(BF16)
    y_own = mm("sr,sk->rk", own_block, w_block)

    rest = after(rest, inverse_block)
    wide = jnp.concatenate([coupling[0, 1], coupling[0, 0], folded(leaf_y)], axis=0)
    gathered = lax.all_gather(after(wide, rest), FRONT, axis=0)
    node_coupling_all = gathered[:, :kp].reshape(K, C)
    leaf_coupling_all = gathered[:, kp : 2 * kp].reshape(K, C)
    leaf_y_all = unfolded(gathered[:, 2 * kp :]).reshape(na, nb, kp, R).transpose(1, 0, 2, 3).reshape(K, R)

    device = jnp.where(place < K, place // kp, (place - K) // kc)
    within = jnp.where(place < K, place % kp, kp + (place - K) % kc)
    section_map = jnp.take(section_all, after(device * ks + within, rest[0]), axis=0)
    section_own = mm("rs,sc->rc", after(own_columns, rest), section_all)

    def section(left, right):
        children = jnp.concatenate([left, right], axis=1)
        return (section_own + mm("rj,jc->rc", children, section_map)).astype(BF16)

    rest = section(from_behind(rest, 1), rest)
    rest = section(from_behind(rest, 1), from_behind(rest, -1))
    left = to_all(from_behind(rest, -(subtree // 2)), FRONT)
    left = left.reshape(na, nb, rc, C).transpose(1, 0, 2, 3).reshape(R, C)

    partial_y = (y_own + mm("rc,ck->rk", left, w_left)).astype(BF16)
    part = total(exchange(partial_y.reshape(na, R // na, K // nb), "fa")).astype(BF16)
    y_block = to_all(part, "fa").reshape(R, K // nb)
    part = mm("bsk,rk->bsr", v_block, y_block).astype(BF16)

    node_reach = mm("pm,mc->pc", after(pivot_inverse[0, 1], y_block), node_coupling_all).astype(BF16)
    leaf_pivots = mm("pk,kr->pr", after(leaf_vectors_pivot[0, 0], y_block), leaf_y_all)
    leaf_pivots = (leaf_pivot_block[0] - leaf_pivots).astype(BF16)
    wide = jnp.concatenate([node_reach, folded(leaf_pivots)], axis=0)
    gathered = lax.all_gather(wide, FRONT, axis=0)
    node_reach_all = gathered[:, :kp].reshape(K, C)
    leaf_pivots_all = unfolded(gathered[:, kp:]).reshape(K, R)
    leaf_reach = mm("pm,mc->pc", pivot_inverse[0, 0], leaf_coupling_all).astype(BF16)
    leaf_own = mm("pm,mr->pr", pivot_inverse[0, 0], leaf_pivots_all)

    placed = mm("sc,rc->sr", own_hit[:, :C].astype(BF16), left)
    reflected = own.astype(F32) + placed - total(exchange(part, "fb"))
    reflected = reflected.astype(BF16)
    remainder = reflected[kp:]
    pivots = to_all(reflected[:kp], "fa").reshape(na * kp, R)
    part = mm("mr,pm->rp", pivots, inverse_block).astype(BF16)
    part = total(exchange(part.reshape(nb, R // nb, nb * kp), "fb")).astype(BF16)
    part = exchange(part.reshape(na, rc, nb * kp), "fa")
    top = part.transpose(1, 0, 2).reshape(rc, K)

    pivot_ids = jnp.arange(K, dtype=jnp.int32)[:, None]
    node_pick = (pivot_ids == parent_columns[0, 1][None]).astype(BF16)
    leaf_pick = (pivot_ids == parent_columns[0, 0][None]).astype(BF16)

    def chosen(parent, pick):
        return mm("rp,pc->rc", parent, pick).astype(BF16)

    node = top
    for height in range(LEVELS, 0, -1):
        if height == LEVELS:
            parent = from_behind(node, subtree // 2)
        else:
            offset = 2 ** (height - 1)
            parent = added(from_behind(node, -offset), from_behind(node, offset))
        node = (top - mm("rc,pc->rp", chosen(parent, node_pick), node_reach_all)).astype(BF16)
    parent = chosen(added(from_behind(node, -1), node), leaf_pick)
    both = node.reshape(rc, fronts, kp).transpose(1, 0, 2)
    both = jnp.concatenate([both, jnp.broadcast_to(parent, (fronts, rc, C))], axis=2)
    both = exchange(both, FRONT).reshape(na, nb, rc, kp + C).transpose(1, 0, 2, 3).reshape(R, kp + C)
    leaf = (leaf_own - mm("pc,rc->pr", leaf_reach, both[:, kp:])).astype(BF16)
    return (jnp.stack([leaf, both[:, :kp].T])[None], remainder[None])


def solution(mesh):
    leaves, fronts = mesh.devices.shape
    nb = next(n for n in range(max(1, int(fronts**0.5)), 0, -1) if fronts % n == 0)
    grid = Mesh(mesh.devices.reshape(leaves, fronts // nb, nb), ("leaf", "fa", "fb"))
    rows3 = P("leaf", FRONT, None)
    rows4 = P("leaf", None, FRONT, None)
    in_specs = (
        *([rows3] * 4),
        *([rows4] * 4),
        P("leaf", None),
        P("leaf", None, None),
        rows4,
        rows4,
    )
    return jax.shard_map(
        per_device, mesh=grid, in_specs=in_specs, out_specs=(rows4, rows3), check_vma=False
    )
```

```python
import jax
import jax.numpy as jnp
from jax import lax
from jax.sharding import Mesh
from jax.sharding import PartitionSpec as P

LEVELS = 2
FRONT = ("fa", "fb")
BF16 = jnp.bfloat16
F32 = jnp.float32


def mm(spec, a, b):
    return jnp.einsum(spec, a, b, preferred_element_type=F32)


def from_behind(block, distance):
    count = lax.axis_size("leaf")
    return lax.ppermute(block, "leaf", [((i - distance) % count, i) for i in range(count)])


def exchange(parts, axis):
    return lax.all_to_all(parts, axis, split_axis=0, concat_axis=0, tiled=True)


def to_all(block, axis):
    count = 1
    for name in (axis,) if isinstance(axis, str) else axis:
        count *= lax.axis_size(name)
    return exchange(jnp.broadcast_to(block, (count, *block.shape)), axis)


def total(parts):
    return jnp.sum(parts.astype(F32), axis=0)


def after(block, earlier):
    corner = earlier[(0,) * (earlier.ndim - 1) + (slice(0, 1),)]
    return block + (corner * 0).astype(block.dtype)


def added(first, second):
    return (first.astype(F32) + second.astype(F32)).astype(BF16)


def folded(block):
    half = block.shape[0] // 2
    return jnp.concatenate([block[:half], block[half:]], axis=1)


def unfolded(blocks):
    half = blocks.shape[-1] // 2
    return jnp.concatenate([blocks[..., :half], blocks[..., half:]], axis=-2)


def per_device(
    leaf_pivot_block,
    leaf_rest_block,
    node_pivot_block,
    node_rest_block,
    leaf_vectors_pivot,
    leaf_vectors_rest,
    node_vectors_pivot,
    node_vectors_rest,
    stack_place,
    parent_columns,
    coupling,
    pivot_inverse,
):
    na, nb = lax.axis_size("fa"), lax.axis_size("fb")
    fronts = na * nb
    ia, ib = lax.axis_index("fa"), lax.axis_index("fb")
    me = ia * nb + ib
    kp = leaf_vectors_pivot.shape[2]
    kc = leaf_vectors_rest.shape[2]
    ks = kp + kc
    K, C = kp * fronts, kc * fronts
    R = leaf_pivot_block.shape[2]
    rc = R // fronts
    place = stack_place[0]
    subtree = 2**LEVELS

    def stack_rows(device):
        device = jnp.asarray(device, jnp.int32)
        return jnp.concatenate(
            [
                device * kp + jnp.arange(kp, dtype=jnp.int32),
                K + device * kc + jnp.arange(kc, dtype=jnp.int32),
            ]
        )

    node_w = jnp.concatenate([node_vectors_pivot[0, 1], node_vectors_rest[0, 1]], axis=0)
    node_v = jnp.concatenate([node_vectors_pivot[0, 0], node_vectors_rest[0, 0]], axis=0)
    rows = stack_rows(me)

    own_hit = rows[:, None] == place[None]
    own = jnp.concatenate([node_pivot_block[0], node_rest_block[0]], axis=0)
    own = jnp.where(jnp.any(own_hit, axis=1)[:, None], jnp.zeros_like(own), own)

    node_ve_all = lax.all_gather(node_vectors_rest[0, 0], FRONT, axis=0, tiled=True)

    leaf_partial = mm("ik,ir->kr", leaf_vectors_pivot[0, 1], leaf_pivot_block[0])
    leaf_partial = leaf_partial + mm("ik,ir->kr", leaf_vectors_rest[0, 1], leaf_rest_block[0])
    part = exchange(leaf_partial.astype(BF16).reshape(nb, K // nb, R), "fb")
    part = exchange(total(part).astype(BF16).reshape(na, kp, R), "fa")
    leaf_y = total(part).astype(BF16)

    both = jnp.concatenate([leaf_rest_block[0], own], axis=0).T.reshape(nb, na, rc, kc + ks)
    leaf_ve = leaf_vectors_rest[0, 0].reshape(kc // rc, rc, nb, na, kp).transpose(2, 3, 1, 0, 4)
    leaf_ve = leaf_ve.reshape(nb, na, rc, kc // rc * kp)
    both = jnp.concatenate([both, leaf_ve], axis=3).transpose(1, 0, 2, 3)
    both = exchange(both.reshape(fronts, rc, both.shape[3]), FRONT)
    leaf_rest = both[:, :, :kc].transpose(1, 0, 2).reshape(rc, C)
    own_columns = both[:, :, kc : kc + ks].transpose(1, 0, 2).reshape(rc, fronts * ks)
    leaf_ve = both[:, :, kc + ks :].reshape(fronts, rc, kc // rc, kp).transpose(0, 2, 1, 3).reshape(C, kp)
    part = mm("kr,ck->rc", leaf_y, leaf_ve).astype(BF16)
    part = part.reshape(nb, na, rc, C).transpose(1, 0, 2, 3).reshape(fronts, rc, C)
    rest = (leaf_rest - total(exchange(part, FRONT))).astype(BF16)

    product = mm("sk,ck->sc", node_w, node_ve_all)
    unit = (rows[:, None] == K + jnp.arange(C, dtype=jnp.int32)[None]).astype(F32)
    section_rows = (after(unit, leaf_y) - product).astype(BF16)

    section_all = lax.all_gather(section_rows, FRONT, axis=0, tiled=True)

    blocks = jnp.concatenate([node_w, node_v], axis=0).reshape(2 * ks, nb, K // nb).transpose(1, 0, 2)
    own_folded = folded(own)
    blocks = jnp.concatenate([blocks, jnp.broadcast_to(own_folded, (nb, *own_folded.shape))], axis=1)
    blocks = exchange(after(blocks, rest), "fb")
    w_block = blocks[:, :ks].reshape(nb * ks, K // nb)
    v_block = blocks[:, ks : 2 * ks]
    own_block = unfolded(blocks[:, 2 * ks :]).reshape(nb * ks, R)

    inverse_block = pivot_inverse[0, 1].reshape(kp, na, nb, kp).transpose(2, 0, 1, 3)
    inverse_block = exchange(inverse_block.reshape(nb, kp, na * kp), "fb")
    inverse_block = inverse_block.reshape(nb * kp, na * kp)
    block_rows = jnp.concatenate([stack_rows(ia * nb + b) for b in range(nb)])
    block_hit = (place[:C, None] == block_rows[None]).astype(BF16)
    w_left = mm("cs,sk->ck", block_hit, w_block).astype(BF16)
    y_own = mm("sr,sk->rk", own_block, w_block)

    rest = after(rest, inverse_block)
    wide = jnp.concatenate([coupling[0, 1], folded(leaf_y)], axis=0)
    gathered = lax.all_gather(after(wide, rest), FRONT, axis=0)
    node_coupling_all = gathered[:, :kp].reshape(K, C)
    leaf_y_all = unfolded(gathered[:, kp:]).reshape(na, nb, kp, R).transpose(1, 0, 2, 3).reshape(K, R)

    device = jnp.where(place < K, place // kp, (place - K) // kc)
    within = jnp.where(place < K, place % kp, kp + (place - K) % kc)
    section_map = jnp.take(section_all, after(device * ks + within, rest[0]), axis=0)
    section_own = mm("rs,sc->rc", after(own_columns, rest), section_all)

    def section(left, right):
        children = jnp.concatenate([left, right], axis=1)
        return (section_own + mm("rj,jc->rc", children, section_map)).astype(BF16)

    rest = section(from_behind(rest, 1), rest)
    rest = section(from_behind(rest, 1), from_behind(rest, -1))
    left = to_all(from_behind(rest, -(subtree // 2)), FRONT)
    left = left.reshape(na, nb, rc, C).transpose(1, 0, 2, 3).reshape(R, C)

    partial_y = (y_own + mm("rc,ck->rk", left, w_left)).astype(BF16)
    part = total(exchange(partial_y.reshape(na, R // na, K // nb), "fa")).astype(BF16)
    node_reach = mm("pm,mc->pc", after(pivot_inverse[0, 1], part), node_coupling_all).astype(BF16)
    leaf_pivots = mm("pk,kr->pr", after(leaf_vectors_pivot[0, 0], part), leaf_y_all)
    leaf_pivots = (leaf_pivot_block[0] - leaf_pivots).astype(BF16)
    wide = jnp.concatenate([node_reach, folded(leaf_pivots)], axis=0)
    gathered = lax.all_gather(wide, FRONT, axis=0)
    node_reach_all = gathered[:, :kp].reshape(K, C)
    leaf_pivots_all = unfolded(gathered[:, kp:]).reshape(K, R)

    y_block = to_all(part, "fa").reshape(R, K // nb)
    part = mm("bsk,rk->bsr", v_block, y_block).astype(BF16)
    placed = mm("sc,rc->sr", own_hit[:, :C].astype(BF16), left)
    reflected = own.astype(F32) + placed - total(exchange(part, "fb"))
    reflected = reflected.astype(BF16)
    remainder = reflected[kp:]
    pivots = to_all(reflected[:kp], "fa").reshape(na * kp, R)
    part = mm("mr,pm->rp", pivots, inverse_block).astype(BF16)
    part = total(exchange(part.reshape(nb, R // nb, nb * kp), "fb")).astype(BF16)
    part = exchange(part.reshape(na, rc, nb * kp), "fa")
    top = part.transpose(1, 0, 2).reshape(rc, K)

    leaf_coupling_all = lax.all_gather(after(coupling[0, 0], node_reach), FRONT, axis=0, tiled=True)
    leaf_reach = mm("pm,mc->pc", pivot_inverse[0, 0], leaf_coupling_all).astype(BF16)
    leaf_own = mm("pm,mr->pr", pivot_inverse[0, 0], leaf_pivots_all)

    pivot_ids = jnp.arange(K, dtype=jnp.int32)[:, None]
    node_pick = (pivot_ids == parent_columns[0, 1][None]).astype(BF16)
    leaf_pick = (pivot_ids == parent_columns[0, 0][None]).astype(BF16)

    def chosen(parent, pick):
        return mm("rp,pc->rc", parent, pick).astype(BF16)

    node = top
    for height in range(LEVELS, 0, -1):
        if height == LEVELS:
            parent = from_behind(node, subtree // 2)
        else:
            offset = 2 ** (height - 1)
            parent = added(from_behind(node, -offset), from_behind(node, offset))
        node = (top - mm("rc,pc->rp", chosen(parent, node_pick), node_reach_all)).astype(BF16)
    parent = chosen(added(from_behind(node, -1), node), leaf_pick)
    both = node.reshape(rc, fronts, kp).transpose(1, 0, 2)
    both = jnp.concatenate([both, jnp.broadcast_to(parent, (fronts, rc, C))], axis=2)
    both = exchange(both, FRONT).reshape(na, nb, rc, kp + C).transpose(1, 0, 2, 3).reshape(R, kp + C)
    leaf = (leaf_own - mm("pc,rc->pr", leaf_reach, both[:, kp:])).astype(BF16)
    return (jnp.stack([leaf, both[:, :kp].T])[None], remainder[None])


def solution(mesh):
    leaves, fronts = mesh.devices.shape
    nb = next(n for n in range(max(1, int(fronts**0.5)), 0, -1) if fronts % n == 0)
    grid = Mesh(mesh.devices.reshape(leaves, fronts // nb, nb), ("leaf", "fa", "fb"))
    rows3 = P("leaf", FRONT, None)
    rows4 = P("leaf", None, FRONT, None)
    in_specs = (
        *([rows3] * 4),
        *([rows4] * 4),
        P("leaf", None),
        P("leaf", None, None),
        rows4,
        rows4,
    )
    return jax.shard_map(
        per_device, mesh=grid, in_specs=in_specs, out_specs=(rows4, rows3), check_vma=False
    )
```
